32 devices in a mesh: replica: 16 (over z, y, core), tensor: 2 (over x).
Axes of the slice: x: 2, y: 2, z: 4, core: 2. Of those that a mesh axis runs over, the one named last changes fastest.
Arguments:
- prefill_q: bfloat16 [6144, 8192], P('replica', 'tensor'), may hold values from -16 to 16
- decode_q: bfloat16 [32, 8192], P('replica', 'tensor'), may hold values from -16 to 16
- overflow_q: bfloat16 [96, 8192], P('replica', 'tensor'), may hold values from -16 to 16
- key_pool: bfloat16 [67584, 1024], P('replica', 'tensor'), may hold values from -10 to 10
- value_pool: bfloat16 [67584, 1024], P('replica', 'tensor'), may hold values from -6 to 6
- prefill_pages: int32 [16, 19], P('replica'), may hold values from 0 to 32, as said below
- decode_pages: int32 [32, 4], P('replica'), may hold values from 0 to 32, as said below
- decode_len: int32 [32], P('replica'), may hold values from 1 to 512, as said below
- overflow_pages: int32 [96], P('replica'), may hold values from 0 to 32, as said below
- overflow_len: int32 [96], P('replica'), may hold values from 1 to 128, as said below
- overflow_dest: int32 [96], P('replica'), may hold values from 0 to 15, as said below
Outputs:
- prefill_out: bfloat16 [6144, 8192], P(('replica', 'tensor'))
- decode_out: bfloat16 [32, 8192], P('replica', 'tensor')
- moved_out: bfloat16 [256, 8192], P('replica', 'tensor')
The draws below stay inside these ranges and needn't reach their ends.
Inputs may be any that keep to these rules, and one draw needn't show every extreme that they name: The page lists of one replica (prefill_pages, decode_pages and overflow_pages together) name distinct pages of that replica's pool. `decode_pages`: distinct pages of the own pool, as for prefill_pages. `overflow_pages`: distinct pages of the own pool, as for prefill_pages. `decode_len`: every replica has a decoding request of exactly 512 positions. `overflow_len`: every replica has an overflow request of exactly 128 positions. `overflow_dest`: the requests of one replica go to distinct replicas other than itself; one replica receives a request from every other replica.
All inputs are finite; a program needn't handle non-finite values.
Results may differ from the reference program's by a relative error of at most 0.0049.
Values may be sent and summed in bfloat16 or wider, within the bound.
No kernel may reach another device: no remote copies, remote signals or barrier semaphores. Data moves between devices by JAX's collectives and lax.ppermute only.
A program may use at most 128 MiB of HBM per device.

```python
import math
import jax
import jax.numpy as jnp
from jax import lax

Q_HEADS = 64
KV_HEADS = 8
D_HEAD = 128
PAGE = 128
STRETCH = 384
PRIOR = 16
DEC = 2
DEC_PAGES = 4
OVERFLOW = 6
PRE_PAGES = 19
POOL = 33
N_REPLICA = 16


def query_draw(key, salt, count):
    noise = 2.5 * jax.random.normal(jax.random.fold_in(key, salt), (count, Q_HEADS * D_HEAD), jnp.float32)
    return jnp.clip(noise, -16.0, 16.0).astype(jnp.bfloat16)


def draw_prefill_q(key, part):
    return query_draw(key, 301, N_REPLICA * STRETCH)


def draw_decode_q(key, part):
    return query_draw(key, 311, N_REPLICA * DEC)


def draw_overflow_q(key, part):
    return query_draw(key, 321, N_REPLICA * OVERFLOW)


def draw_key_pool(key, part):
    total = N_REPLICA * POOL * PAGE
    noise = jax.random.normal(jax.random.fold_in(key, 201), (total, KV_HEADS * D_HEAD), jnp.float32)
    return jnp.clip(noise, -10.0, 10.0).astype(jnp.bfloat16)


def pool_orders(key):
    seeds = jax.random.split(jax.random.fold_in(key, 11), N_REPLICA)
    return jax.vmap(lambda k: jax.random.permutation(k, POOL))(seeds).astype(jnp.int32)


def draw_prefill_pages(key, part):
    return pool_orders(key)[:, :PRE_PAGES]


def draw_decode_pages(key, part):
    return pool_orders(key)[:, PRE_PAGES:PRE_PAGES + DEC * DEC_PAGES].reshape(N_REPLICA * DEC, DEC_PAGES)


def draw_overflow_pages(key, part):
    return pool_orders(key)[:, PRE_PAGES + DEC * DEC_PAGES:].reshape(N_REPLICA * OVERFLOW)


def ragged(key, salt, count, most):
    base = jax.random.randint(jax.random.fold_in(key, salt), (N_REPLICA, count), 1, most + 1)
    spot = jax.random.randint(jax.random.fold_in(key, salt + 1), (N_REPLICA, 1), 0, count)
    filled = jnp.where(jnp.arange(count)[None, :] == spot, most, base)
    return filled.reshape(-1).astype(jnp.int32)


def draw_decode_len(key, part):
    return ragged(key, 21, DEC, DEC_PAGES * PAGE)


def draw_overflow_len(key, part):
    return ragged(key, 25, OVERFLOW, PAGE)


def draw_overflow_dest(key, part):
    busiest = jax.random.randint(jax.random.fold_in(key, 31), (), 0, N_REPLICA)
    source = jnp.arange(N_REPLICA, dtype=jnp.int32)
    seeds = jax.random.split(jax.random.fold_in(key, 32), N_REPLICA)
    offsets = jax.vmap(lambda k: jax.random.permutation(k, N_REPLICA - 1))(seeds).astype(jnp.int32)
    forced = ((busiest - source - 1) % N_REPLICA)[:, None]
    column = jnp.arange(N_REPLICA - 1, dtype=jnp.int32)[None, :]
    place = jax.random.randint(jax.random.fold_in(key, 33), (N_REPLICA, 1), 0, OVERFLOW)
    displaced = jnp.take_along_axis(offsets, place, axis=1)
    swapped = jnp.where(offsets == forced, displaced, jnp.where(column == place, forced, offsets))
    chosen = jnp.where((source == busiest)[:, None], offsets, swapped)[:, :OVERFLOW]
    return ((source[:, None] + 1 + chosen) % N_REPLICA).reshape(-1).astype(jnp.int32)


def block_scale(stream_key, extent, pieces, low, largest):
    loudness, own = 1.0, jax.random.fold_in(stream_key, 6)
    for position, shards_of in pieces:
        steps = jnp.exp(jax.random.uniform(jax.random.fold_in(own, position), (shards_of,), jnp.float32, low / len(pieces), largest / len(pieces)))
        loudness = loudness * jnp.repeat(steps, extent[position] // shards_of).reshape([-1 if axis == position else 1 for axis in range(len(extent))])
    return loudness


def centred(own_key, shape, scale, most, pieces=(), kind=jnp.bfloat16):
    gain = block_scale(own_key, shape, pieces, -0.22, 0.18) if pieces else 1.0
    array = jax.random.normal(own_key, shape, jnp.float32) * scale * gain
    return jnp.minimum(jnp.maximum(array, -most), most).astype(kind)


def setup_inputs(seed: int = 0) -> dict:
    key_of = jax.random.split(jax.random.key(seed), 12)
    return {
        "prefill_q": draw_prefill_q(jax.random.fold_in(key_of[11], 71), 0),
        "decode_q": draw_decode_q(jax.random.fold_in(key_of[11], 71), 0),
        "overflow_q": draw_overflow_q(jax.random.fold_in(key_of[11], 71), 0),
        "key_pool": draw_key_pool(jax.random.fold_in(key_of[11], 71), 0),
        "value_pool": centred(key_of[4], (N_REPLICA * POOL * PAGE, KV_HEADS * D_HEAD), 1.0, 6.0, ((0, 16), (1, 2))),
        "prefill_pages": draw_prefill_pages(jax.random.fold_in(key_of[11], 71), 0),
        "decode_pages": draw_decode_pages(jax.random.fold_in(key_of[11], 71), 0),
        "decode_len": draw_decode_len(jax.random.fold_in(key_of[11], 71), 0),
        "overflow_pages": draw_overflow_pages(jax.random.fold_in(key_of[11], 71), 0),
        "overflow_len": draw_overflow_len(jax.random.fold_in(key_of[11], 71), 0),
        "overflow_dest": draw_overflow_dest(jax.random.fold_in(key_of[11], 71), 0),
    }


def attend_block(queries, key_rows, value_rows, usable):
    per_group = Q_HEADS // KV_HEADS
    count = queries.shape[0]
    q_four = queries.astype(jnp.float32).reshape(count, KV_HEADS, per_group, D_HEAD)
    k_three = key_rows.astype(jnp.float32).reshape(-1, KV_HEADS, D_HEAD)
    v_three = value_rows.astype(jnp.float32).reshape(-1, KV_HEADS, D_HEAD)
    scores = jnp.einsum('ngqd,lgd->gqnl', q_four, k_three) / math.sqrt(D_HEAD)
    scores = jnp.where(usable[None, None], scores, -1e+30)
    maxima = lax.optimization_barrier(jnp.max(scores, axis=-1, keepdims=True))
    expon = jnp.exp(scores - maxima)
    weights = (expon / lax.optimization_barrier(jnp.sum(expon, axis=-1, keepdims=True))).astype(jnp.bfloat16)
    result = jnp.einsum('gqnl,lgd->ngqd', weights.astype(jnp.float32), v_three)
    return result.reshape(count, -1).astype(jnp.bfloat16)

def attend_single(query_row, key_rows, value_rows, usable):
    return attend_block(query_row[None], key_rows, value_rows, usable[None])[0]

def reference(prefill_q, decode_q, overflow_q, key_pool, value_pool, prefill_pages, decode_pages, decode_len, overflow_pages, overflow_len, overflow_dest):
    width_kv = KV_HEADS * D_HEAD
    width_q = Q_HEADS * D_HEAD
    key_parts = key_pool.reshape(N_REPLICA, POOL, PAGE, width_kv)
    value_parts = value_pool.reshape(N_REPLICA, POOL, PAGE, width_kv)
    key_span = PRE_PAGES * PAGE
    causal = jnp.arange(key_span)[None, :] <= (PRIOR * PAGE + jnp.arange(STRETCH))[:, None]

    def prefill_replica(inputs):
        queries, key_pages, value_pages, page_list = inputs
        key_rows = key_pages[page_list].reshape(key_span, width_kv)
        value_rows = value_pages[page_list].reshape(key_span, width_kv)
        return attend_block(queries, key_rows, value_rows, causal)
    prefill_out = lax.map(prefill_replica, (prefill_q.reshape(N_REPLICA, STRETCH, width_q), key_parts, value_parts, prefill_pages))
    prefill_out = prefill_out.reshape(N_REPLICA * STRETCH, width_q)

    def decode_replica(inputs):
        queries, key_pages, value_pages, listed_pages, lengths = inputs
        key_rows = key_pages[listed_pages].reshape(DEC, DEC_PAGES * PAGE, width_kv)
        value_rows = value_pages[listed_pages].reshape(DEC, DEC_PAGES * PAGE, width_kv)
        usable = jnp.arange(DEC_PAGES * PAGE)[None, :] < lengths[:, None]
        return jax.vmap(attend_single)(queries, key_rows, value_rows, usable)
    decode_out = lax.map(decode_replica, (decode_q.reshape(N_REPLICA, DEC, width_q), key_parts, value_parts, decode_pages.reshape(N_REPLICA, DEC, DEC_PAGES), decode_len.reshape(N_REPLICA, DEC)))
    decode_out = decode_out.reshape(N_REPLICA * DEC, width_q)

    def overflow_replica(inputs):
        queries, key_pages, value_pages, page_ids, lengths = inputs
        key_rows = key_pages[page_ids]
        value_rows = value_pages[page_ids]
        usable = jnp.arange(PAGE)[None, :] < lengths[:, None]
        return jax.vmap(attend_single)(queries, key_rows, value_rows, usable)
    moved = lax.map(overflow_replica, (overflow_q.reshape(N_REPLICA, OVERFLOW, width_q), key_parts, value_parts, overflow_pages.reshape(N_REPLICA, OVERFLOW), overflow_len.reshape(N_REPLICA, OVERFLOW)))
    target = overflow_dest.reshape(N_REPLICA, OVERFLOW) * N_REPLICA + jnp.arange(N_REPLICA, dtype=jnp.int32)[:, None]
    moved_out = jnp.zeros((N_REPLICA * N_REPLICA, width_q), jnp.bfloat16)
    moved_out = moved_out.at[target.reshape(-1).astype(jnp.int32)].set(moved.reshape(-1, width_q))
    return (prefill_out, decode_out, moved_out)
```

```python
import functools
import math

import jax
import jax.numpy as jnp
from jax import lax
from jax.experimental import pallas as pl
from jax.experimental.pallas import tpu as pltpu
from jax.sharding import PartitionSpec as P

Q_HEADS = 64
KV_HEADS = 8
D_HEAD = 128
PAGE = 128
GROUP = Q_HEADS // KV_HEADS
SCALE = math.log2(math.e) / math.sqrt(D_HEAD)
LOW = -1e30
CHUNK = 512

NT = (((1,), (1,)), ((), ()))


def prefill_kernel(
    tail, blk_ref, pages_ref, q_ref, k_hbm, v_hbm, o_ref, kbuf, vbuf, acc, peak, sem, *, first
):
    step, steps = pl.program_id(0), pl.num_programs(0)
    count = pages_ref.shape[0]
    span = count * PAGE
    rows = q_ref.shape[0]
    earlier = span - tail

    def fetch(head):
        cols = pl.ds(pl.multiple_of((first + head) * D_HEAD, D_HEAD), D_HEAD)

        def one(j, _):
            src = pl.ds(pl.multiple_of(pages_ref[j] * PAGE, PAGE), PAGE)
            dst = pl.ds(pl.multiple_of(j * PAGE, PAGE), PAGE)
            pltpu.make_async_copy(k_hbm.at[src, cols], kbuf.at[head, dst], sem.at[head, 0]).start()
            pltpu.make_async_copy(v_hbm.at[src, cols], vbuf.at[head, dst], sem.at[head, 1]).start()
            return 0

        lax.fori_loop(0, count, one, 0)

    @pl.when(step == 0)
    def _():
        fetch(0)

    @pl.when(step + 1 < steps)
    def _():
        fetch(step + 1)

    acc[...] = jnp.zeros_like(acc)
    peak[...] = jnp.full_like(peak, LOW)
    q = jnp.concatenate([q_ref[:, h * D_HEAD:(h + 1) * D_HEAD] for h in range(GROUP)], axis=0)
    pltpu.make_async_copy(kbuf.at[step], kbuf.at[step], sem.at[step, 0]).wait()
    pltpu.make_async_copy(vbuf.at[step], vbuf.at[step], sem.at[step, 1]).wait()

    def absorb(start, size, usable=None):
        keys = kbuf[step, pl.ds(start, size), :]
        values = vbuf[step, pl.ds(start, size), :]
        s = lax.dot_general(q, keys, NT, preferred_element_type=jnp.float32)
        if usable is not None:
            s = jnp.where(usable[None], s.reshape(GROUP, rows, size), LOW).reshape(GROUP * rows, size)
        before = peak[...]
        after = jnp.maximum(before, jnp.max(s, axis=1, keepdims=True))
        shift = after * SCALE
        p = jnp.exp2(s * SCALE - jnp.concatenate([shift] * (size // D_HEAD), axis=1))
        wide = jnp.concatenate([values, jnp.ones_like(values)], axis=1)
        o = jnp.dot(p.astype(jnp.bfloat16), wide, preferred_element_type=jnp.float32)
        fade = jnp.exp2(before * SCALE - shift)
        acc[...] = acc[...] * jnp.concatenate([fade, fade], axis=1) + o
        peak[...] = after

    whole = earlier // CHUNK

    def body(j, _):
        absorb(pl.multiple_of(j * CHUNK, CHUNK), CHUNK)
        return 0

    lax.fori_loop(0, whole, body, 0)
    if earlier > whole * CHUNK:
        absorb(whole * CHUNK, earlier - whole * CHUNK)
    limit = blk_ref[0] * rows + lax.broadcasted_iota(jnp.int32, (rows, tail), 0)
    absorb(earlier, tail, lax.broadcasted_iota(jnp.int32, (rows, tail), 1) <= limit)
    o = (acc[:, :D_HEAD] / acc[:, D_HEAD:]).astype(o_ref.dtype)
    for h in range(GROUP):
        o_ref[:, h * D_HEAD:(h + 1) * D_HEAD] = o[h * rows:(h + 1) * rows]


def prefill_part(q, keys, values, pages, blk, ranks, first, heads, wide=False):
    tokens = q.shape[0]
    rows = tokens // ranks
    span = pages.shape[0] * PAGE
    width = GROUP * D_HEAD
    total = (ranks * keys.shape[1] // D_HEAD) if wide else heads
    work = heads * GROUP * rows * span
    here = keys.shape[1] // D_HEAD

    def place(g, blk, pages):
        return (0, blk[0] * here + first + g) if wide else (0, g)

    return pl.pallas_call(
        functools.partial(prefill_kernel, tokens, first=first),
        grid_spec=pltpu.PrefetchScalarGridSpec(
            num_scalar_prefetch=2,
            grid=(heads,),
            in_specs=[
                pl.BlockSpec((rows, width), lambda g, blk, pages: (blk[0], first + g)),
                pl.BlockSpec(memory_space=pl.ANY),
                pl.BlockSpec(memory_space=pl.ANY),
            ],
            out_specs=pl.BlockSpec((rows, width), place),
            scratch_shapes=[
                pltpu.VMEM((heads, span, D_HEAD), jnp.bfloat16),
                pltpu.VMEM((heads, span, D_HEAD), jnp.bfloat16),
                pltpu.VMEM((GROUP * rows, 2 * D_HEAD), jnp.float32),
                pltpu.VMEM((GROUP * rows, D_HEAD), jnp.float32),
                pltpu.SemaphoreType.DMA((heads, 2)),
            ],
        ),
        out_shape=jax.ShapeDtypeStruct((rows, total * width), q.dtype),
        compiler_params=pltpu.CompilerParams(vmem_limit_bytes=48 * 2**20),
        cost_estimate=pl.CostEstimate(
            flops=4 * work * D_HEAD,
            bytes_accessed=4 * heads * (span * D_HEAD + rows * width),
            transcendentals=work,
        ),
        name="prefill",
    )(blk, pages, q, keys, values)


def small_kernel(
    dec, over, pages_ref, len_ref, dest_ref, q_ref, k_hbm, v_hbm, dec_ref, mov_ref,
    kbuf, vbuf, res, moved, sem
):
    count = pages_ref.shape[0]
    batch = q_ref.shape[0]
    per = (count - over) // dec
    keys = count * PAGE

    def one(j, _):
        src = pl.ds(pl.multiple_of(pages_ref[j] * PAGE, PAGE), PAGE)
        dst = pl.ds(pl.multiple_of(j * PAGE, PAGE), PAGE)
        pltpu.make_async_copy(k_hbm.at[src], kbuf.at[dst], sem.at[0]).start()
        pltpu.make_async_copy(v_hbm.at[src], vbuf.at[dst], sem.at[1]).start()
        return 0

    lax.fori_loop(0, count, one, 0)
    moved[...] = jnp.zeros_like(moved)
    row = lax.broadcasted_iota(jnp.int32, (batch, PAGE), 0)
    lane = lax.broadcasted_iota(jnp.int32, (batch, PAGE), 1)
    masks = []
    for j in range(count):
        owner, base = (j // per, j % per * PAGE) if j < dec * per else (j - dec * per + dec, 0)
        masks.append((row == owner) & (lane + base < len_ref[owner]))
    pltpu.make_async_copy(kbuf, kbuf, sem.at[0]).wait()
    pltpu.make_async_copy(vbuf, vbuf, sem.at[1]).wait()
    for g in range(k_hbm.shape[1] // D_HEAD):
        cols = slice(g * D_HEAD, (g + 1) * D_HEAD)
        q = jnp.concatenate(
            [q_ref[:, (g * GROUP + h) * D_HEAD:(g * GROUP + h + 1) * D_HEAD] for h in range(GROUP)],
            axis=0,
        ).astype(jnp.bfloat16)
        s = lax.dot_general(q, kbuf[:, cols], NT, preferred_element_type=jnp.float32)
        s = s.reshape(GROUP, batch, keys)
        s = jnp.concatenate(
            [
                jnp.where(masks[j][None], s[:, :, j * PAGE:(j + 1) * PAGE], LOW)
                for j in range(count)
            ],
            axis=2,
        ).reshape(GROUP * batch, keys)
        p = jnp.exp2((s - jnp.max(s, axis=1, keepdims=True)) * SCALE)
        total = jnp.sum(p, axis=1, keepdims=True)
        w = (p / total).astype(jnp.bfloat16)
        o = jnp.dot(w, vbuf[:, cols], preferred_element_type=jnp.float32)
        for h in range(GROUP):
            at = (g * GROUP + h) * D_HEAD
            res[:, at:at + D_HEAD] = o[h * batch:(h + 1) * batch]
    dec_ref[...] = res[0:dec, :].astype(dec_ref.dtype)
    for m in range(over):
        moved[pl.ds(dest_ref[m], 1), :] = res[dec + m:dec + m + 1, :]
    mov_ref[...] = moved[...].astype(mov_ref.dtype)


def small_part(decode_q, overflow_q, keys, values, pages, lens, dest, replicas):
    dec, over = decode_q.shape[0], overflow_q.shape[0]
    batch = -(-(dec + over) // 8) * 8
    width = decode_q.shape[1]
    q = jnp.concatenate([decode_q, overflow_q], axis=0).astype(jnp.float32)
    q = jnp.pad(q, ((0, batch - dec - over), (0, 0)))
    span = pages.shape[0] * PAGE
    work = batch * width * span
    return pl.pallas_call(
        functools.partial(small_kernel, dec, over),
        grid_spec=pltpu.PrefetchScalarGridSpec(
            num_scalar_prefetch=3,
            grid=(1,),
            in_specs=[
                pl.BlockSpec((batch, width), lambda i, *_: (0, 0)),
                pl.BlockSpec(memory_space=pl.ANY),
                pl.BlockSpec(memory_space=pl.ANY),
            ],
            out_specs=[
                pl.BlockSpec((dec, width), lambda i, *_: (0, 0)),
                pl.BlockSpec((replicas, width), lambda i, *_: (0, 0)),
            ],
            scratch_shapes=[
                pltpu.VMEM((span, keys.shape[1]), jnp.bfloat16),
                pltpu.VMEM((span, keys.shape[1]), jnp.bfloat16),
                pltpu.VMEM((batch, width), jnp.float32),
                pltpu.VMEM((replicas, width), jnp.float32),
                pltpu.SemaphoreType.DMA((2,)),
            ],
        ),
        out_shape=[
            jax.ShapeDtypeStruct((dec, width), decode_q.dtype),
            jax.ShapeDtypeStruct((replicas, width), decode_q.dtype),
        ],
        compiler_params=pltpu.CompilerParams(vmem_limit_bytes=48 * 2**20),
        cost_estimate=pl.CostEstimate(
            flops=4 * work, bytes_accessed=4 * span * keys.shape[1], transcendentals=work // D_HEAD
        ),
        name="small",
    )(pages, lens, dest, q, keys, values)


def per_device(
    prefill_q,
    decode_q,
    overflow_q,
    key_pool,
    value_pool,
    prefill_pages,
    decode_pages,
    decode_len,
    overflow_pages,
    overflow_len,
    overflow_dest,
):
    ranks, replicas = lax.axis_size("tensor"), lax.axis_size("replica")
    rank = lax.axis_index("tensor")
    heads = key_pool.shape[1] // D_HEAD
    cols = GROUP * D_HEAD
    pages = prefill_pages[0]

    decode_out, sent = small_part(
        decode_q,
        overflow_q,
        key_pool,
        value_pool,
        jnp.concatenate([decode_pages.reshape(-1), overflow_pages]),
        jnp.concatenate([decode_len, overflow_len]),
        overflow_dest,
        replicas,
    )
    moved_out = lax.all_to_all(sent, "replica", split_axis=0, concat_axis=0, tiled=True)

    arrived = []
    for shift in range(1, ranks):
        blk = lax.rem(rank + shift, ranks)[None].astype(jnp.int32)
        source = lax.rem(rank + ranks - shift, ranks)
        for g in range(heads):
            part = prefill_part(prefill_q, key_pool, value_pool, pages, blk, ranks, g, 1)
            got = lax.ppermute(part, "tensor", [(i, (i + shift) % ranks) for i in range(ranks)])
            arrived.append((source * heads * cols + g * cols, got))
    prefill_out = prefill_part(
        prefill_q, key_pool, value_pool, pages, rank[None].astype(jnp.int32), ranks, 0, heads, wide=True
    )
    for at, got in arrived:
        prefill_out = lax.dynamic_update_slice(prefill_out, got, (0, at))
    return (prefill_out, decode_out, moved_out)


def solution(mesh):
    in_specs = (
        P("replica", "tensor"),
        P("replica", "tensor"),
        P("replica", "tensor"),
        P("replica", "tensor"),
        P("replica", "tensor"),
        P("replica", None),
        P("replica", None),
        P("replica"),
        P("replica"),
        P("replica"),
        P("replica"),
    )
    out_specs = (P(("replica", "tensor"), None), P("replica", "tensor"), P("replica", "tensor"))
    return jax.shard_map(
        per_device, mesh=mesh, in_specs=in_specs, out_specs=out_specs, check_vma=False
    )
```

```python
import functools
import math

import jax
import jax.numpy as jnp
from jax import lax
from jax.experimental import pallas as pl
from jax.experimental.pallas import tpu as pltpu
from jax.sharding import PartitionSpec as P

Q_HEADS = 64
KV_HEADS = 8
D_HEAD = 128
PAGE = 128
GROUP = Q_HEADS // KV_HEADS
SCALE = math.log2(math.e) / math.sqrt(D_HEAD)
LOW = -1e30
BOUND = 2.0**100
CHUNK = 512
VMEM_LIMIT = 60 * 2**20

NT = (((1,), (1,)), ((), ()))


def chunks_of(earlier, tail):
    starts = list(range(0, earlier, CHUNK)) + [earlier]
    return [(a, b - a) for a, b in zip(starts, starts[1:] + [earlier + tail])]


def prefill_kernel(
    tail, blk_ref, pages_ref, q_ref, k_hbm, v_hbm, o_ref, kbuf, vbuf, acc, peak, sem, *, first
):
    step, steps = pl.program_id(0), pl.num_programs(0)
    count = pages_ref.shape[0]
    span = count * PAGE
    rows = q_ref.shape[0]
    pieces = chunks_of(span - tail, tail)

    def fetch(head):
        cols = pl.ds(pl.multiple_of((first + head) * D_HEAD, D_HEAD), D_HEAD)
        for i, (start, size) in enumerate(pieces):

            def one(j, _):
                src = pl.ds(pl.multiple_of(pages_ref[j] * PAGE, PAGE), PAGE)
                dst = pl.ds(pl.multiple_of(j * PAGE, PAGE), PAGE)
                pltpu.make_async_copy(
                    k_hbm.at[src, cols], kbuf.at[head, dst], sem.at[head, i, 0]
                ).start()
                pltpu.make_async_copy(
                    v_hbm.at[src, cols], vbuf.at[head, dst], sem.at[head, i, 1]
                ).start()
                return 0

            lax.fori_loop(start // PAGE, (start + size) // PAGE, one, 0)

    @pl.when(step == 0)
    def _():
        fetch(0)

    @pl.when(step + 1 < steps)
    def _():
        fetch(step + 1)

    q = jnp.concatenate([q_ref[:, h * D_HEAD:(h + 1) * D_HEAD] for h in range(GROUP)], axis=0)

    def wait(buf, i, kind):
        part = buf.at[step, pl.ds(*pieces[i])]
        pltpu.make_async_copy(part, part, sem.at[step, i, kind]).wait()

    def scores(start, size):
        keys = kbuf[step, pl.ds(start, size), :]
        return lax.dot_general(q, keys, NT, preferred_element_type=jnp.float32)

    def mixed(p, start, size):
        values = vbuf[step, pl.ds(start, size), :]
        wide = jnp.concatenate([values, jnp.ones_like(values)], axis=1)
        return jnp.dot(p.astype(jnp.bfloat16), wide, preferred_element_type=jnp.float32)

    def across(x, size):
        return jnp.concatenate([x] * (size // D_HEAD), axis=1)

    def masked(x, start, size):
        limit = span - tail - start + blk_ref[0] * rows
        usable = lax.broadcasted_iota(jnp.int32, (rows, size), 1) <= (
            lax.broadcasted_iota(jnp.int32, (rows, size), 0) + limit
        )
        return jnp.where(usable[None], x.reshape(GROUP, rows, size), LOW).reshape(x.shape)

    wait(kbuf, 0, 0)
    s = scores(*pieces[0])
    for i, (start, size) in enumerate(pieces):
        if i + 1 < len(pieces):
            wait(kbuf, i + 1, 0)
            later = scores(*pieces[i + 1])
        if i == 0:
            top = jnp.max(s, axis=1, keepdims=True) * SCALE
            peak[...] = jnp.broadcast_to(top, peak.shape)
        x = s * SCALE - across(peak[...], size)
        if start >= span - tail:
            x = masked(x, start, size)
        p = jnp.exp2(x)
        wait(vbuf, i, 1)
        o = mixed(p, start, size)
        acc[...] = o if i == 0 else acc[...] + o
        s = later

    fine = jnp.min(jnp.where(acc[:, D_HEAD:] < BOUND, 1.0, 0.0))

    @pl.when(fine < 0.5)
    def _():
        acc[...] = jnp.zeros_like(acc)
        peak[...] = jnp.full_like(peak, LOW)

        def body(j, _):
            start = pl.multiple_of(j * PAGE, PAGE)
            s = masked(scores(start, PAGE) * SCALE, start, PAGE)
            before = peak[...]
            after = jnp.maximum(before, jnp.max(s, axis=1, keepdims=True))
            o = mixed(jnp.exp2(s - after), start, PAGE)
            acc[...] = acc[...] * across(jnp.exp2(before - after), 2 * D_HEAD) + o
            peak[...] = after
            return 0

        lax.fori_loop(0, count, body, 0)

    o = (acc[:, :D_HEAD] / acc[:, D_HEAD:]).astype(o_ref.dtype)
    for h in range(GROUP):
        o_ref[:, h * D_HEAD:(h + 1) * D_HEAD] = o[h * rows:(h + 1) * rows]


def prefill_part(q, keys, values, pages, blk, ranks, first, heads, wide=False):
    tokens = q.shape[0]
    rows = tokens // ranks
    span = pages.shape[0] * PAGE
    width = GROUP * D_HEAD
    total = (ranks * keys.shape[1] // D_HEAD) if wide else heads
    work = heads * GROUP * rows * span
    here = keys.shape[1] // D_HEAD

    def place(g, blk, pages):
        return (0, blk[0] * here + first + g) if wide else (0, g)

    return pl.pallas_call(
        functools.partial(prefill_kernel, tokens, first=first),
        grid_spec=pltpu.PrefetchScalarGridSpec(
            num_scalar_prefetch=2,
            grid=(heads,),
            in_specs=[
                pl.BlockSpec((rows, width), lambda g, blk, pages: (blk[0], first + g)),
                pl.BlockSpec(memory_space=pl.ANY),
                pl.BlockSpec(memory_space=pl.ANY),
            ],
            out_specs=pl.BlockSpec((rows, width), place),
            scratch_shapes=[
                pltpu.VMEM((heads, span, D_HEAD), jnp.bfloat16),
                pltpu.VMEM((heads, span, D_HEAD), jnp.bfloat16),
                pltpu.VMEM((GROUP * rows, 2 * D_HEAD), jnp.float32),
                pltpu.VMEM((GROUP * rows, D_HEAD), jnp.float32),
                pltpu.SemaphoreType.DMA((heads, len(chunks_of(span - tokens, tokens)), 2)),
            ],
        ),
        out_shape=jax.ShapeDtypeStruct((rows, total * width), q.dtype),
        compiler_params=pltpu.CompilerParams(vmem_limit_bytes=VMEM_LIMIT),
        cost_estimate=pl.CostEstimate(
            flops=4 * work * D_HEAD,
            bytes_accessed=4 * heads * (span * D_HEAD + rows * width),
            transcendentals=work,
        ),
        name="prefill",
    )(blk, pages, q, keys, values)


def small_kernel(
    dec, over, pages_ref, len_ref, dest_ref, q_ref, k_hbm, v_hbm, dec_ref, out_ref,
    kbuf, vbuf, res, sem
):
    count = pages_ref.shape[0]
    batch = q_ref.shape[0]
    per = (count - over) // dec
    keys = count * PAGE

    def one(j, _):
        src = pl.ds(pl.multiple_of(pages_ref[j] * PAGE, PAGE), PAGE)
        dst = pl.ds(pl.multiple_of(j * PAGE, PAGE), PAGE)
        pltpu.make_async_copy(k_hbm.at[src], kbuf.at[dst], sem.at[0]).start()
        pltpu.make_async_copy(v_hbm.at[src], vbuf.at[dst], sem.at[1]).start()
        return 0

    lax.fori_loop(0, count, one, 0)
    row = lax.broadcasted_iota(jnp.int32, (batch, PAGE), 0)
    lane = lax.broadcasted_iota(jnp.int32, (batch, PAGE), 1)
    masks = []
    for j in range(count):
        owner, base = (j, 0) if j < over else (over + (j - over) // per, (j - over) % per * PAGE)
        masks.append((row == owner) & (lane + base < len_ref[owner]))
    pltpu.make_async_copy(kbuf, kbuf, sem.at[0]).wait()
    pltpu.make_async_copy(vbuf, vbuf, sem.at[1]).wait()
    for g in range(k_hbm.shape[1] // D_HEAD):
        cols = slice(g * D_HEAD, (g + 1) * D_HEAD)
        q = jnp.concatenate(
            [q_ref[:, (g * GROUP + h) * D_HEAD:(g * GROUP + h + 1) * D_HEAD] for h in range(GROUP)],
            axis=0,
        ).astype(jnp.bfloat16)
        s = lax.dot_general(q, kbuf[:, cols], NT, preferred_element_type=jnp.float32)
        s = s.reshape(GROUP, batch, keys)
        s = jnp.concatenate(
            [
                jnp.where(masks[j][None], s[:, :, j * PAGE:(j + 1) * PAGE], LOW)
                for j in range(count)
            ],
            axis=2,
        ).reshape(GROUP * batch, keys)
        p = jnp.exp2((s - jnp.max(s, axis=1, keepdims=True)) * SCALE)
        total = jnp.sum(p, axis=1, keepdims=True)
        w = (p / total).astype(jnp.bfloat16)
        o = jnp.dot(w, vbuf[:, cols], preferred_element_type=jnp.float32)
        for h in range(GROUP):
            at = (g * GROUP + h) * D_HEAD
            res[:, at:at + D_HEAD] = o[h * batch:(h + 1) * batch]
    width = q_ref.shape[1]
    dec_ref[...] = res[over:over + dec, :].astype(dec_ref.dtype)
    lines = out_ref.shape[0]
    line = lax.broadcasted_iota(jnp.int32, (lines, D_HEAD), 0)
    where_to = jnp.full((lines, D_HEAD), -1, jnp.int32)
    for m in range(over):
        where_to = jnp.where(line == m, dest_ref[m], where_to)
    out_ref[:, width:] = where_to.astype(jnp.float32).astype(out_ref.dtype)
    real = lax.broadcasted_iota(jnp.int32, (lines, width), 0) < over
    out_ref[:, :width] = jnp.where(real, res[0:lines, :], 0.0).astype(out_ref.dtype)


def small_part(decode_q, overflow_q, keys, values, pages, lens, dest):
    dec, over = decode_q.shape[0], overflow_q.shape[0]
    lines = -(-over // 8) * 8
    batch = -(-(dec + over) // 8) * 8
    width = decode_q.shape[1]
    q = jnp.concatenate([overflow_q, decode_q], axis=0).astype(jnp.float32)
    q = jnp.pad(q, ((0, batch - dec - over), (0, 0)))
    span = pages.shape[0] * PAGE
    work = batch * width * span
    return pl.pallas_call(
        functools.partial(small_kernel, dec, over),
        grid_spec=pltpu.PrefetchScalarGridSpec(
            num_scalar_prefetch=3,
            grid=(1,),
            in_specs=[
                pl.BlockSpec((batch, width), lambda i, *_: (0, 0)),
                pl.BlockSpec(memory_space=pl.ANY),
                pl.BlockSpec(memory_space=pl.ANY),
            ],
            out_specs=[
                pl.BlockSpec((dec, width), lambda i, *_: (0, 0)),
                pl.BlockSpec((lines, width + D_HEAD), lambda i, *_: (0, 0)),
            ],
            scratch_shapes=[
                pltpu.VMEM((span, keys.shape[1]), jnp.bfloat16),
                pltpu.VMEM((span, keys.shape[1]), jnp.bfloat16),
                pltpu.VMEM((batch, width), jnp.float32),
                pltpu.SemaphoreType.DMA((2,)),
            ],
        ),
        out_shape=[
            jax.ShapeDtypeStruct((dec, width), decode_q.dtype),
            jax.ShapeDtypeStruct((lines, width + D_HEAD), decode_q.dtype),
        ],
        compiler_params=pltpu.CompilerParams(vmem_limit_bytes=VMEM_LIMIT),
        cost_estimate=pl.CostEstimate(
            flops=4 * work, bytes_accessed=4 * span * keys.shape[1], transcendentals=work // D_HEAD
        ),
        name="small",
    )(pages, lens, dest, q, keys, values)


def finish_kernel(me_ref, at_ref, all_ref, big_ref, *refs):
    got, (out_ref, mov_ref, sem) = refs[:-3], refs[-3:]
    del big_ref
    cols = GROUP * D_HEAD
    copies = []
    for i, part in enumerate(got):
        to = pl.ds(pl.multiple_of(at_ref[i] * cols, cols), cols)
        copies.append(pltpu.make_async_copy(part, out_ref.at[:, to], sem.at[i]))
        copies[-1].start()
    replicas, width = mov_ref.shape
    lines = all_ref.shape[1]
    table = all_ref[...].astype(jnp.float32).reshape(replicas * lines, width + D_HEAD)
    mine = table[:, width:width + 1] == me_ref[0].astype(jnp.float32)
    row = lax.broadcasted_iota(jnp.int32, (replicas * lines, replicas), 0)
    col = lax.broadcasted_iota(jnp.int32, (replicas * lines, replicas), 1)
    ours = mine & (row >= col * lines) & (row < (col + 1) * lines)
    pick = jnp.where(ours, 1.0, 0.0).astype(jnp.bfloat16)
    mov_ref[...] = lax.dot_general(
        pick,
        table[:, :width].astype(jnp.bfloat16),
        (((0,), (0,)), ((), ())),
        preferred_element_type=jnp.float32,
    ).astype(mov_ref.dtype)
    for copy in copies:
        copy.wait()


def finish_part(me, at, everyone, big, got):
    replicas, lines, width = everyone.shape
    width -= D_HEAD
    anywhere = pl.BlockSpec(memory_space=pl.ANY)
    return pl.pallas_call(
        finish_kernel,
        grid_spec=pltpu.PrefetchScalarGridSpec(
            num_scalar_prefetch=2,
            grid=(1,),
            in_specs=[pl.BlockSpec(everyone.shape, lambda i, *_: (0, 0, 0)), anywhere]
            + [anywhere] * len(got),
            out_specs=[anywhere, pl.BlockSpec((replicas, width), lambda i, *_: (0, 0))],
            scratch_shapes=[pltpu.SemaphoreType.DMA((len(got),))],
        ),
        out_shape=[
            jax.ShapeDtypeStruct(big.shape, big.dtype),
            jax.ShapeDtypeStruct((replicas, width), big.dtype),
        ],
        input_output_aliases={3: 0},
        compiler_params=pltpu.CompilerParams(vmem_limit_bytes=VMEM_LIMIT),
        cost_estimate=pl.CostEstimate(
            flops=0, bytes_accessed=2 * big.size + 2 * everyone.size, transcendentals=0
        ),
        name="finish",
    )(me, at, everyone, big, *got)


def per_device(
    prefill_q,
    decode_q,
    overflow_q,
    key_pool,
    value_pool,
    prefill_pages,
    decode_pages,
    decode_len,
    overflow_pages,
    overflow_len,
    overflow_dest,
):
    ranks = lax.axis_size("tensor")
    rank = lax.axis_index("tensor")
    heads = key_pool.shape[1] // D_HEAD
    pages = prefill_pages[0]

    decode_out, sent = small_part(
        decode_q,
        overflow_q,
        key_pool,
        value_pool,
        jnp.concatenate([overflow_pages, decode_pages.reshape(-1)]),
        jnp.concatenate([overflow_len, decode_len]),
        overflow_dest,
    )
    everyone = lax.all_gather(sent, "replica", axis=0, tiled=False)

    got, at = [], []
    for shift in range(1, ranks):
        blk = lax.rem(rank + shift, ranks)[None].astype(jnp.int32)
        source = lax.rem(rank + ranks - shift, ranks)
        for g in range(heads):
            part = prefill_part(prefill_q, key_pool, value_pool, pages, blk, ranks, g, 1)
            got.append(lax.ppermute(part, "tensor", [(i, (i + shift) % ranks) for i in range(ranks)]))
            at.append(source * heads + g)
    prefill_out = prefill_part(
        prefill_q, key_pool, value_pool, pages, rank[None].astype(jnp.int32), ranks, 0, heads, wide=True
    )
    me = lax.axis_index("replica")[None].astype(jnp.int32)
    prefill_out, moved_out = finish_part(
        me, jnp.stack(at).astype(jnp.int32), everyone, prefill_out, got
    )
    return (prefill_out, decode_out, moved_out)


def solution(mesh):
    in_specs = (
        P("replica", "tensor"),
        P("replica", "tensor"),
        P("replica", "tensor"),
        P("replica", "tensor"),
        P("replica", "tensor"),
        P("replica", None),
        P("replica", None),
        P("replica"),
        P("replica"),
        P("replica"),
        P("replica"),
    )
    out_specs = (P(("replica", "tensor"), None), P("replica", "tensor"), P("replica", "tensor"))
    return jax.shard_map(
        per_device, mesh=mesh, in_specs=in_specs, out_specs=out_specs, check_vma=False
    )
```

```python
import functools
import math

import jax
import jax.numpy as jnp
from jax import lax
from jax.experimental import pallas as pl
from jax.experimental.pallas import tpu as pltpu
from jax.sharding import PartitionSpec as P

Q_HEADS = 64
KV_HEADS = 8
D_HEAD = 128
PAGE = 128
GROUP = Q_HEADS // KV_HEADS
SCALE = math.log2(math.e) / math.sqrt(D_HEAD)
LOW = -1e30
CHUNK = 512
PACK = 2
VMEM_LIMIT = 60 * 2**20

NT = (((1,), (1,)), ((), ()))


def chunks_of(earlier, tail):
    starts = list(range(0, earlier, CHUNK)) + [earlier]
    return [(a, b - a) for a, b in zip(starts, starts[1:] + [earlier + tail])]


def prefill_kernel(
    tail, blk_ref, pages_ref, q_ref, k_hbm, v_hbm, o_ref,
    kbuf, vbuf, score_a, score_b, top_a, top_b, sem, *, first
):
    heads = kbuf.shape[0]
    count = pages_ref.shape[0]
    span = count * PAGE
    rows = q_ref.shape[0]
    units = GROUP // PACK
    pieces = chunks_of(span - tail, tail)

    def fetch(head):
        cols = pl.ds(pl.multiple_of((first + head) * D_HEAD, D_HEAD), D_HEAD)

        def one(j, _):
            src = pl.ds(pl.multiple_of(pages_ref[j] * PAGE, PAGE), PAGE)
            dst = pl.ds(pl.multiple_of(j * PAGE, PAGE), PAGE)
            pltpu.make_async_copy(k_hbm.at[src, cols], kbuf.at[head, dst], sem.at[head, 0]).start()
            pltpu.make_async_copy(v_hbm.at[src, cols], vbuf.at[head, dst], sem.at[head, 1]).start()
            return 0

        lax.fori_loop(0, count, one, 0)

    def ready(head):
        pltpu.make_async_copy(kbuf.at[head], kbuf.at[head], sem.at[head, 0]).wait()
        pltpu.make_async_copy(vbuf.at[head], vbuf.at[head], sem.at[head, 1]).wait()

    def columns(unit, h):
        return pl.ds(pl.multiple_of((unit * PACK + h) * D_HEAD, D_HEAD), D_HEAD)

    def across(x, size):
        return jnp.concatenate([x] * (size // D_HEAD), axis=1)

    def run(now, later):
        if later is not None:
            unit, score, top = later
            head = unit // units
            q = jnp.concatenate([q_ref[:, columns(unit, h)] for h in range(PACK)], axis=0)
            best = None
        if now is not None:
            unit_now, score_now, top_now = now
            head_now = unit_now // units
            shift = top_now[...]
            acc = None
        for start, size in pieces:
            if later is not None:
                keys = kbuf[head, start:start + size, :]
                s = lax.dot_general(q, keys, NT, preferred_element_type=jnp.float32)
                if start >= span - tail:
                    usable = lax.broadcasted_iota(jnp.int32, (rows, size), 1) <= (
                        lax.broadcasted_iota(jnp.int32, (rows, size), 0) + blk_ref[0] * rows
                    )
                    s = jnp.where(usable[None], s.reshape(PACK, rows, size), LOW).reshape(s.shape)
                score[:, start:start + size] = s
                for at in range(0, size, D_HEAD):
                    piece = s[:, at:at + D_HEAD]
                    best = piece if best is None else jnp.maximum(best, piece)
            if now is not None:
                p = jnp.exp2(score_now[:, start:start + size] * SCALE - across(shift, size))
                values = vbuf[head_now, start:start + size, :]
                wide = jnp.concatenate([values, jnp.ones_like(values)], axis=1)
                o = jnp.dot(p.astype(jnp.bfloat16), wide, preferred_element_type=jnp.float32)
                acc = o if acc is None else acc + o
        if later is not None:
            top[...] = jnp.broadcast_to(jnp.max(best, axis=1, keepdims=True) * SCALE, top.shape)
        if now is not None:
            o = (acc[:, :D_HEAD] / acc[:, D_HEAD:]).astype(o_ref.dtype)
            for h in range(PACK):
                o_ref[:, columns(unit_now, h)] = o[h * rows:(h + 1) * rows]

    fetch(0)
    if heads > 1:
        fetch(1)
    ready(0)
    a, b = (score_a, top_a), (score_b, top_b)
    run(None, (0, *a))

    def body(i, _):
        u = 2 * i
        run((u, *a), (u + 1, *b))
        if heads > 1:
            head = (u + 2) // units

            @pl.when(((u + 2) % units == 0) & (head < heads))
            def _():
                @pl.when(head + 1 < heads)
                def _():
                    fetch(head + 1)

                ready(head)

        run((u + 1, *b), (jnp.minimum(u + 2, heads * units - 1), *a))
        return 0

    lax.fori_loop(0, heads * units // 2, body, 0)


def prefill_part(q, keys, values, pages, blk, ranks, first, heads, wide=False):
    tokens = q.shape[0]
    rows = tokens // ranks
    span = pages.shape[0] * PAGE
    width = heads * GROUP * D_HEAD
    total = ranks * keys.shape[1] // D_HEAD // heads if wide else 1
    work = heads * GROUP * rows * span

    return pl.pallas_call(
        functools.partial(prefill_kernel, tokens, first=first),
        grid_spec=pltpu.PrefetchScalarGridSpec(
            num_scalar_prefetch=2,
            grid=(1,),
            in_specs=[
                pl.BlockSpec((rows, width), lambda i, blk, pages: (blk[0], first // heads)),
                pl.BlockSpec(memory_space=pl.ANY),
                pl.BlockSpec(memory_space=pl.ANY),
            ],
            out_specs=pl.BlockSpec((rows, width), lambda i, blk, pages: (0, blk[0] if wide else 0)),
            scratch_shapes=[
                pltpu.VMEM((heads, span, D_HEAD), jnp.bfloat16),
                pltpu.VMEM((heads, span, D_HEAD), jnp.bfloat16),
                pltpu.VMEM((PACK * rows, span), jnp.float32),
                pltpu.VMEM((PACK * rows, span), jnp.float32),
                pltpu.VMEM((PACK * rows, D_HEAD), jnp.float32),
                pltpu.VMEM((PACK * rows, D_HEAD), jnp.float32),
                pltpu.SemaphoreType.DMA((heads, 2)),
            ],
        ),
        out_shape=jax.ShapeDtypeStruct((rows, total * width), q.dtype),
        compiler_params=pltpu.CompilerParams(vmem_limit_bytes=VMEM_LIMIT),
        cost_estimate=pl.CostEstimate(
            flops=4 * work * D_HEAD,
            bytes_accessed=4 * (heads * span * D_HEAD + rows * width),
            transcendentals=work,
        ),
        name="prefill",
    )(blk, pages, q, keys, values)


def small_kernel(
    dec, over, pages_ref, len_ref, dest_ref, q_ref, k_hbm, v_hbm, dec_ref, out_ref,
    kbuf, vbuf, res, sem
):
    count = pages_ref.shape[0]
    batch = q_ref.shape[0]
    per = (count - over) // dec
    keys = count * PAGE

    def one(j, _):
        src = pl.ds(pl.multiple_of(pages_ref[j] * PAGE, PAGE), PAGE)
        dst = pl.ds(pl.multiple_of(j * PAGE, PAGE), PAGE)
        pltpu.make_async_copy(k_hbm.at[src], kbuf.at[dst], sem.at[0]).start()
        pltpu.make_async_copy(v_hbm.at[src], vbuf.at[dst], sem.at[1]).start()
        return 0

    lax.fori_loop(0, count, one, 0)
    row = lax.broadcasted_iota(jnp.int32, (batch, PAGE), 0)
    lane = lax.broadcasted_iota(jnp.int32, (batch, PAGE), 1)
    masks = []
    for j in range(count):
        owner, base = (j, 0) if j < over else (over + (j - over) // per, (j - over) % per * PAGE)
        masks.append((row == owner) & (lane + base < len_ref[owner]))
    pltpu.make_async_copy(kbuf, kbuf, sem.at[0]).wait()
    pltpu.make_async_copy(vbuf, vbuf, sem.at[1]).wait()
    for g in range(k_hbm.shape[1] // D_HEAD):
        cols = slice(g * D_HEAD, (g + 1) * D_HEAD)
        q = jnp.concatenate(
            [q_ref[:, (g * GROUP + h) * D_HEAD:(g * GROUP + h + 1) * D_HEAD] for h in range(GROUP)],
            axis=0,
        ).astype(jnp.bfloat16)
        s = lax.dot_general(q, kbuf[:, cols], NT, preferred_element_type=jnp.float32)
        s = s.reshape(GROUP, batch, keys)
        s = jnp.concatenate(
            [
                jnp.where(masks[j][None], s[:, :, j * PAGE:(j + 1) * PAGE], LOW)
                for j in range(count)
            ],
            axis=2,
        ).reshape(GROUP * batch, keys)
        p = jnp.exp2((s - jnp.max(s, axis=1, keepdims=True)) * SCALE)
        total = jnp.sum(p, axis=1, keepdims=True)
        w = (p / total).astype(jnp.bfloat16)
        o = jnp.dot(w, vbuf[:, cols], preferred_element_type=jnp.float32)
        for h in range(GROUP):
            at = (g * GROUP + h) * D_HEAD
            res[:, at:at + D_HEAD] = o[h * batch:(h + 1) * batch]
    width = q_ref.shape[1]
    dec_ref[...] = res[over:over + dec, :].astype(dec_ref.dtype)
    lines = out_ref.shape[0]
    line = lax.broadcasted_iota(jnp.int32, (lines, D_HEAD), 0)
    where_to = jnp.full((lines, D_HEAD), -1, jnp.int32)
    for m in range(over):
        where_to = jnp.where(line == m, dest_ref[m], where_to)
    out_ref[:, width:] = where_to.astype(jnp.float32).astype(out_ref.dtype)
    real = lax.broadcasted_iota(jnp.int32, (lines, width), 0) < over
    out_ref[:, :width] = jnp.where(real, res[0:lines, :], 0.0).astype(out_ref.dtype)


def small_part(decode_q, overflow_q, keys, values, pages, lens, dest):
    dec, over = decode_q.shape[0], overflow_q.shape[0]
    lines = -(-over // 8) * 8
    batch = -(-(dec + over) // 8) * 8
    width = decode_q.shape[1]
    q = jnp.concatenate([overflow_q, decode_q], axis=0).astype(jnp.float32)
    q = jnp.pad(q, ((0, batch - dec - over), (0, 0)))
    span = pages.shape[0] * PAGE
    work = batch * width * span
    return pl.pallas_call(
        functools.partial(small_kernel, dec, over),
        grid_spec=pltpu.PrefetchScalarGridSpec(
            num_scalar_prefetch=3,
            grid=(1,),
            in_specs=[
                pl.BlockSpec((batch, width), lambda i, *_: (0, 0)),
                pl.BlockSpec(memory_space=pl.ANY),
                pl.BlockSpec(memory_space=pl.ANY),
            ],
            out_specs=[
                pl.BlockSpec((dec, width), lambda i, *_: (0, 0)),
                pl.BlockSpec((lines, width + D_HEAD), lambda i, *_: (0, 0)),
            ],
            scratch_shapes=[
                pltpu.VMEM((span, keys.shape[1]), jnp.bfloat16),
                pltpu.VMEM((span, keys.shape[1]), jnp.bfloat16),
                pltpu.VMEM((batch, width), jnp.float32),
                pltpu.SemaphoreType.DMA((2,)),
            ],
        ),
        out_shape=[
            jax.ShapeDtypeStruct((dec, width), decode_q.dtype),
            jax.ShapeDtypeStruct((lines, width + D_HEAD), decode_q.dtype),
        ],
        compiler_params=pltpu.CompilerParams(vmem_limit_bytes=VMEM_LIMIT),
        cost_estimate=pl.CostEstimate(
            flops=4 * work, bytes_accessed=4 * span * keys.shape[1], transcendentals=work // D_HEAD
        ),
        name="small",
    )(pages, lens, dest, q, keys, values)


def finish_kernel(me_ref, at_ref, all_ref, big_ref, *refs):
    got, (out_ref, mov_ref, sem) = refs[:-3], refs[-3:]
    del big_ref
    cols = GROUP * D_HEAD
    copies = []
    for i, part in enumerate(got):
        to = pl.ds(pl.multiple_of(at_ref[i] * cols, cols), cols)
        copies.append(pltpu.make_async_copy(part, out_ref.at[:, to], sem.at[i]))
        copies[-1].start()
    replicas, width = mov_ref.shape
    lines = all_ref.shape[1]
    table = all_ref[...].astype(jnp.float32).reshape(replicas * lines, width + D_HEAD)
    mine = table[:, width:width + 1] == me_ref[0].astype(jnp.float32)
    row = lax.broadcasted_iota(jnp.int32, (replicas * lines, replicas), 0)
    col = lax.broadcasted_iota(jnp.int32, (replicas * lines, replicas), 1)
    ours = mine & (row >= col * lines) & (row < (col + 1) * lines)
    pick = jnp.where(ours, 1.0, 0.0).astype(jnp.bfloat16)
    mov_ref[...] = lax.dot_general(
        pick,
        table[:, :width].astype(jnp.bfloat16),
        (((0,), (0,)), ((), ())),
        preferred_element_type=jnp.float32,
    ).astype(mov_ref.dtype)
    for copy in copies:
        copy.wait()


def finish_part(me, at, everyone, big, got):
    replicas, lines, width = everyone.shape
    width -= D_HEAD
    anywhere = pl.BlockSpec(memory_space=pl.ANY)
    return pl.pallas_call(
        finish_kernel,
        grid_spec=pltpu.PrefetchScalarGridSpec(
            num_scalar_prefetch=2,
            grid=(1,),
            in_specs=[pl.BlockSpec(everyone.shape, lambda i, *_: (0, 0, 0)), anywhere]
            + [pl.BlockSpec(memory_space=pltpu.VMEM)] * len(got),
            out_specs=[anywhere, pl.BlockSpec((replicas, width), lambda i, *_: (0, 0))],
            scratch_shapes=[pltpu.SemaphoreType.DMA((len(got),))],
        ),
        out_shape=[
            jax.ShapeDtypeStruct(big.shape, big.dtype),
            jax.ShapeDtypeStruct((replicas, width), big.dtype),
        ],
        input_output_aliases={3: 0},
        compiler_params=pltpu.CompilerParams(vmem_limit_bytes=VMEM_LIMIT),
        cost_estimate=pl.CostEstimate(
            flops=0, bytes_accessed=2 * big.size + 2 * everyone.size, transcendentals=0
        ),
        name="finish",
    )(me, at, everyone, big, *got)


def per_device(
    prefill_q,
    decode_q,
    overflow_q,
    key_pool,
    value_pool,
    prefill_pages,
    decode_pages,
    decode_len,
    overflow_pages,
    overflow_len,
    overflow_dest,
):
    ranks = lax.axis_size("tensor")
    rank = lax.axis_index("tensor")
    heads = key_pool.shape[1] // D_HEAD
    pages = prefill_pages[0]

    decode_out, sent = small_part(
        decode_q,
        overflow_q,
        key_pool,
        value_pool,
        jnp.concatenate([overflow_pages, decode_pages.reshape(-1)]),
        jnp.concatenate([overflow_len, decode_len]),
        overflow_dest,
    )
    everyone = lax.all_gather(sent, "replica", axis=0, tiled=False)

    got, at = [], []
    for shift in range(1, ranks):
        blk = lax.rem(rank + shift, ranks)[None].astype(jnp.int32)
        source = lax.rem(rank + ranks - shift, ranks)
        for g in range(heads):
            part = prefill_part(prefill_q, key_pool, value_pool, pages, blk, ranks, g, 1)
            got.append(lax.ppermute(part, "tensor", [(i, (i + shift) % ranks) for i in range(ranks)]))
            at.append(source * heads + g)
    prefill_out = prefill_part(
        prefill_q, key_pool, value_pool, pages, rank[None].astype(jnp.int32), ranks, 0, heads, wide=True
    )
    me = lax.axis_index("replica")[None].astype(jnp.int32)
    prefill_out, moved_out = finish_part(
        me, jnp.stack(at).astype(jnp.int32), everyone, prefill_out, got
    )
    return (prefill_out, decode_out, moved_out)


def solution(mesh):
    in_specs = (
        P("replica", "tensor"),
        P("replica", "tensor"),
        P("replica", "tensor"),
        P("replica", "tensor"),
        P("replica", "tensor"),
        P("replica", None),
        P("replica", None),
        P("replica"),
        P("replica"),
        P("replica"),
        P("replica"),
    )
    out_specs = (P(("replica", "tensor"), None), P("replica", "tensor"), P("replica", "tensor"))
    return jax.shard_map(
        per_device, mesh=mesh, in_specs=in_specs, out_specs=out_specs, check_vma=False
    )
```

```python
import functools
import math

import jax
import jax.numpy as jnp
from jax import lax
from jax.experimental import pallas as pl
from jax.experimental.pallas import tpu as pltpu
from jax.sharding import PartitionSpec as P

Q_HEADS = 64
KV_HEADS = 8
D_HEAD = 128
PAGE = 128
GROUP = Q_HEADS // KV_HEADS
SCALE = math.log2(math.e) / math.sqrt(D_HEAD)
LOW = -1e30
CHUNK = 512
VMEM_LIMIT = 60 * 2**20

NT = (((1,), (1,)), ((), ()))


def chunks_of(earlier, tail):
    starts = list(range(0, earlier, CHUNK)) + [earlier]
    return [(a, b - a) for a, b in zip(starts, starts[1:] + [earlier + tail])]


def prefill_kernel(
    tail, blk_ref, pages_ref, q_ref, k_hbm, v_hbm, o_ref,
    kbuf, vbuf, turned, score_a, score_b, top_a, top_b, sem, *, first, pack, turn
):
    heads = kbuf.shape[0]
    count = pages_ref.shape[0]
    span = count * PAGE
    rows = q_ref.shape[0]
    units = GROUP // pack
    pieces = chunks_of(span - tail, tail)

    def fetch(head):
        cols = pl.ds(pl.multiple_of((first + head) * D_HEAD, D_HEAD), D_HEAD)

        def one(j, _):
            src = pl.ds(pl.multiple_of(pages_ref[j] * PAGE, PAGE), PAGE)
            dst = pl.ds(pl.multiple_of(j * PAGE, PAGE), PAGE)
            pltpu.make_async_copy(k_hbm.at[src, cols], kbuf.at[head, dst], sem.at[head, 0]).start()
            pltpu.make_async_copy(v_hbm.at[src, cols], vbuf.at[head, dst], sem.at[head, 1]).start()
            return 0

        lax.fori_loop(0, count, one, 0)

    def keys_ready(head):
        pltpu.make_async_copy(kbuf.at[head], kbuf.at[head], sem.at[head, 0]).wait()
        if turn:

            def one(j, _):
                at = pl.ds(pl.multiple_of(j * PAGE, PAGE), PAGE)
                turned[:, at] = kbuf[head, at, :].T
                return 0

            lax.fori_loop(0, count, one, 0)

    def values_ready(head):
        pltpu.make_async_copy(vbuf.at[head], vbuf.at[head], sem.at[head, 1]).wait()

    def columns(unit, h):
        return pl.ds(pl.multiple_of((unit * pack + h) * D_HEAD, D_HEAD), D_HEAD)

    def across(x, size):
        return jnp.concatenate([x] * (size // D_HEAD), axis=1)

    def run(now, later):
        if later is not None:
            unit, score, top = later
            head = unit // units
            q = jnp.concatenate([q_ref[:, columns(unit, h)] for h in range(pack)], axis=0)
            best = None
        if now is not None:
            unit_now, score_now, top_now = now
            head_now = unit_now // units
            shift = top_now[...]
            acc = None
        for start, size in pieces:
            if later is not None:
                if turn:
                    s = jnp.dot(
                        q, turned[:, start:start + size], preferred_element_type=jnp.float32
                    )
                else:
                    keys = kbuf[head, start:start + size, :]
                    s = lax.dot_general(q, keys, NT, preferred_element_type=jnp.float32)
                if start >= span - tail:
                    usable = lax.broadcasted_iota(jnp.int32, (rows, size), 1) <= (
                        lax.broadcasted_iota(jnp.int32, (rows, size), 0) + blk_ref[0] * rows
                    )
                    s = jnp.where(usable[None], s.reshape(pack, rows, size), LOW).reshape(s.shape)
                score[:, start:start + size] = s
                for at in range(0, size, D_HEAD):
                    piece = s[:, at:at + D_HEAD]
                    best = piece if best is None else jnp.maximum(best, piece)
            if now is not None:
                p = jnp.exp2(score_now[:, start:start + size] * SCALE - across(shift, size))
                values = vbuf[head_now, start:start + size, :]
                wide = jnp.concatenate([values, jnp.ones_like(values)], axis=1)
                o = jnp.dot(p.astype(jnp.bfloat16), wide, preferred_element_type=jnp.float32)
                acc = o if acc is None else acc + o
        if later is not None:
            top[...] = jnp.broadcast_to(jnp.max(best, axis=1, keepdims=True) * SCALE, top.shape)
        if now is not None:
            o = (acc[:, :D_HEAD] / acc[:, D_HEAD:]).astype(o_ref.dtype)
            for h in range(pack):
                o_ref[:, columns(unit_now, h)] = o[h * rows:(h + 1) * rows]

    fetch(0)
    if heads > 1:
        fetch(1)
    keys_ready(0)
    a, b = (score_a, top_a), (score_b, top_b)
    run(None, (0, *a))
    values_ready(0)

    def body(i, _):
        u = 2 * i
        run((u, *a), (u + 1, *b))
        if heads > 1:
            head = (u + 2) // units

            @pl.when((u + 2) % units == 0)
            def _():
                @pl.when(head + 1 < heads)
                def _():
                    fetch(head + 1)

                keys_ready(head)
                values_ready(head)

        run((u + 1, *b), (u + 2, *a))
        return 0

    last = heads * units
    lax.fori_loop(0, last // 2 - 1, body, 0)
    run((last - 2, *a), (last - 1, *b))
    run((last - 1, *b), None)


def prefill_part(q, keys, values, pages, blk, ranks, first, heads, pack, turn, wide=False):
    tokens = q.shape[0]
    rows = tokens // ranks
    span = pages.shape[0] * PAGE
    width = heads * GROUP * D_HEAD
    total = ranks * keys.shape[1] // D_HEAD // heads if wide else 1
    work = heads * GROUP * rows * span

    return pl.pallas_call(
        functools.partial(prefill_kernel, tokens, first=first, pack=pack, turn=turn),
        grid_spec=pltpu.PrefetchScalarGridSpec(
            num_scalar_prefetch=2,
            grid=(1,),
            in_specs=[
                pl.BlockSpec((rows, width), lambda i, blk, pages: (blk[0], first // heads)),
                pl.BlockSpec(memory_space=pl.ANY),
                pl.BlockSpec(memory_space=pl.ANY),
            ],
            out_specs=pl.BlockSpec((rows, width), lambda i, blk, pages: (0, blk[0] if wide else 0)),
            scratch_shapes=[
                pltpu.VMEM((heads, span, D_HEAD), jnp.bfloat16),
                pltpu.VMEM((heads, span, D_HEAD), jnp.bfloat16),
                pltpu.VMEM((D_HEAD, span), jnp.bfloat16),
                pltpu.VMEM((pack * rows, span), jnp.float32),
                pltpu.VMEM((pack * rows, span), jnp.float32),
                pltpu.VMEM((pack * rows, D_HEAD), jnp.float32),
                pltpu.VMEM((pack * rows, D_HEAD), jnp.float32),
                pltpu.SemaphoreType.DMA((heads, 2)),
            ],
        ),
        out_shape=jax.ShapeDtypeStruct((rows, total * width), q.dtype),
        compiler_params=pltpu.CompilerParams(vmem_limit_bytes=VMEM_LIMIT),
        cost_estimate=pl.CostEstimate(
            flops=4 * work * D_HEAD,
            bytes_accessed=4 * (heads * span * D_HEAD + rows * width),
            transcendentals=work,
        ),
        name="prefill",
    )(blk, pages, q, keys, values)


def small_kernel(
    over_pages, dec_pages, over_len, dec_len, dest_ref, over_ref, decq_ref, k_hbm, v_hbm,
    dec_ref, out_ref, kbuf, vbuf, q_all, res, flat, sem
):
    over, (dec, per) = over_pages.shape[0], dec_pages.shape
    count = over + dec * per
    batch = q_all.shape[0]
    keys = count * PAGE
    heads = q_all.shape[1] // D_HEAD

    for j in range(count):
        page = over_pages[j] if j < over else dec_pages[(j - over) // per, (j - over) % per]
        src = pl.ds(pl.multiple_of(page * PAGE, PAGE), PAGE)
        dst = pl.ds(j * PAGE, PAGE)
        pltpu.make_async_copy(k_hbm.at[src], kbuf.at[dst], sem.at[0]).start()
        pltpu.make_async_copy(v_hbm.at[src], vbuf.at[dst], sem.at[1]).start()

    if batch > over + dec:
        q_all[...] = jnp.zeros_like(q_all)
    q_all[0:over, :] = over_ref[...].astype(jnp.float32)
    q_all[over:over + dec, :] = decq_ref[...].astype(jnp.float32)
    out_ref[...] = jnp.zeros_like(out_ref)
    row = lax.broadcasted_iota(jnp.int32, (batch, PAGE), 0)
    lane = lax.broadcasted_iota(jnp.int32, (batch, PAGE), 1)
    masks = []
    for j in range(count):
        owner, base = (j, 0) if j < over else (over + (j - over) // per, (j - over) % per * PAGE)
        most = over_len[j] if j < over else dec_len[owner - over]
        masks.append((row == owner) & (lane + base < most))
    pltpu.make_async_copy(kbuf, kbuf, sem.at[0]).wait()
    for g in range(k_hbm.shape[1] // D_HEAD):
        cols = slice(g * D_HEAD, (g + 1) * D_HEAD)
        q = jnp.concatenate(
            [q_all[:, (g * GROUP + h) * D_HEAD:(g * GROUP + h + 1) * D_HEAD] for h in range(GROUP)],
            axis=0,
        ).astype(jnp.bfloat16)
        s = lax.dot_general(q, kbuf[:, cols], NT, preferred_element_type=jnp.float32)
        s = s.reshape(GROUP, batch, keys)
        s = jnp.concatenate(
            [
                jnp.where(masks[j][None], s[:, :, j * PAGE:(j + 1) * PAGE], LOW)
                for j in range(count)
            ],
            axis=2,
        ).reshape(GROUP * batch, keys)
        p = jnp.exp2((s - jnp.max(s, axis=1, keepdims=True)) * SCALE)
        total = jnp.sum(p, axis=1, keepdims=True)
        w = (p / total).astype(jnp.bfloat16)
        if g == 0:
            pltpu.make_async_copy(vbuf, vbuf, sem.at[1]).wait()
        o = jnp.dot(w, vbuf[:, cols], preferred_element_type=jnp.float32)
        for h in range(GROUP):
            at = g * GROUP + h
            res[:, at * D_HEAD:(at + 1) * D_HEAD] = o[h * batch:(h + 1) * batch]
            flat[pl.ds(at, batch, stride=heads), :] = o[h * batch:(h + 1) * batch]
    dec_ref[...] = res[over:over + dec, :].astype(dec_ref.dtype)
    for m in range(over):
        out_ref[dest_ref[m]] = flat[m * heads:(m + 1) * heads, :].astype(out_ref.dtype)


def small_part(decode_q, overflow_q, keys, values, dec_pages, over_pages, dec_len, over_len, dest, replicas):
    dec, over = decode_q.shape[0], overflow_q.shape[0]
    batch = -(-(dec + over) // 8) * 8
    width = decode_q.shape[1]
    span = (over + dec_pages.size) * PAGE
    work = batch * width * span
    moved = (replicas, width // D_HEAD, D_HEAD)
    return pl.pallas_call(
        small_kernel,
        grid_spec=pltpu.PrefetchScalarGridSpec(
            num_scalar_prefetch=5,
            grid=(1,),
            in_specs=[
                pl.BlockSpec((over, width), lambda i, *_: (0, 0)),
                pl.BlockSpec((dec, width), lambda i, *_: (0, 0)),
                pl.BlockSpec(memory_space=pl.ANY),
                pl.BlockSpec(memory_space=pl.ANY),
            ],
            out_specs=[
                pl.BlockSpec((dec, width), lambda i, *_: (0, 0)),
                pl.BlockSpec(moved, lambda i, *_: (0, 0, 0)),
            ],
            scratch_shapes=[
                pltpu.VMEM((span, keys.shape[1]), jnp.bfloat16),
                pltpu.VMEM((span, keys.shape[1]), jnp.bfloat16),
                pltpu.VMEM((batch, width), jnp.float32),
                pltpu.VMEM((batch, width), jnp.float32),
                pltpu.VMEM((batch * width // D_HEAD, D_HEAD), jnp.float32),
                pltpu.SemaphoreType.DMA((2,)),
            ],
        ),
        out_shape=[
            jax.ShapeDtypeStruct((dec, width), decode_q.dtype),
            jax.ShapeDtypeStruct(moved, decode_q.dtype),
        ],
        compiler_params=pltpu.CompilerParams(vmem_limit_bytes=VMEM_LIMIT),
        cost_estimate=pl.CostEstimate(
            flops=4 * work, bytes_accessed=4 * span * keys.shape[1], transcendentals=work // D_HEAD
        ),
        name="small",
    )(over_pages, dec_pages, over_len, dec_len, dest, overflow_q, decode_q, keys, values)


def finish_kernel(ranks, rank_ref, rows_ref, big_ref, *refs):
    got, (out_ref, mov_ref, flat, sem) = refs[:-4], refs[-4:]
    del big_ref
    cols = GROUP * D_HEAD
    heads = len(got) // (ranks - 1)
    copies = []
    for i, part in enumerate(got):
        source = lax.rem(rank_ref[0] + ranks - (i // heads + 1), ranks)
        to = pl.ds(pl.multiple_of((source * heads + i % heads) * cols, cols), cols)
        copies.append(pltpu.make_async_copy(part, out_ref.at[:, to], sem.at[i]))
        copies[-1].start()
    replicas, count, _ = rows_ref.shape
    flat[...] = rows_ref[...].astype(jnp.float32).reshape(flat.shape)
    for h in range(count):
        line = flat[pl.ds(h, replicas, stride=count), :]
        mov_ref[:, h * D_HEAD:(h + 1) * D_HEAD] = line.astype(mov_ref.dtype)
    for copy in copies:
        copy.wait()


def finish_part(rank, ranks, rows, big, got):
    replicas, count, _ = rows.shape
    anywhere = pl.BlockSpec(memory_space=pl.ANY)
    return pl.pallas_call(
        functools.partial(finish_kernel, ranks),
        grid_spec=pltpu.PrefetchScalarGridSpec(
            num_scalar_prefetch=1,
            grid=(1,),
            in_specs=[pl.BlockSpec(rows.shape, lambda i, *_: (0, 0, 0)), anywhere]
            + [pl.BlockSpec(memory_space=pltpu.VMEM)] * len(got),
            out_specs=[anywhere, pl.BlockSpec((replicas, count * D_HEAD), lambda i, *_: (0, 0))],
            scratch_shapes=[
                pltpu.VMEM((replicas * count, D_HEAD), jnp.float32),
                pltpu.SemaphoreType.DMA((len(got),)),
            ],
        ),
        out_shape=[
            jax.ShapeDtypeStruct(big.shape, big.dtype),
            jax.ShapeDtypeStruct((replicas, count * D_HEAD), big.dtype),
        ],
        input_output_aliases={2: 0},
        compiler_params=pltpu.CompilerParams(vmem_limit_bytes=VMEM_LIMIT),
        cost_estimate=pl.CostEstimate(
            flops=0, bytes_accessed=2 * big.size + 4 * rows.size, transcendentals=0
        ),
        name="finish",
    )(rank, rows, big, *got)


def per_device(
    prefill_q,
    decode_q,
    overflow_q,
    key_pool,
    value_pool,
    prefill_pages,
    decode_pages,
    decode_len,
    overflow_pages,
    overflow_len,
    overflow_dest,
):
    ranks, replicas = lax.axis_size("tensor"), lax.axis_size("replica")
    rank = lax.axis_index("tensor")
    heads = key_pool.shape[1] // D_HEAD
    pages = prefill_pages[0]

    decode_out, sent = small_part(
        decode_q,
        overflow_q,
        key_pool,
        value_pool,
        decode_pages,
        overflow_pages,
        decode_len,
        overflow_len,
        overflow_dest,
        replicas,
    )
    rows = lax.all_to_all(sent, "replica", split_axis=0, concat_axis=0, tiled=True)

    got = []
    for shift in range(1, ranks):
        blk = lax.rem(rank + shift, ranks)[None].astype(jnp.int32)
        for g in range(heads):
            part = prefill_part(
                prefill_q, key_pool, value_pool, pages, blk, ranks, g, 1, pack=2, turn=True
            )
            got.append(lax.ppermute(part, "tensor", [(i, (i + shift) % ranks) for i in range(ranks)]))
    own = rank[None].astype(jnp.int32)
    prefill_out = prefill_part(
        prefill_q, key_pool, value_pool, pages, own, ranks, 0, heads, pack=4, turn=False, wide=True
    )
    prefill_out, moved_out = finish_part(own, ranks, rows, prefill_out, got)
    return (prefill_out, decode_out, moved_out)


def solution(mesh):
    in_specs = (
        P("replica", "tensor"),
        P("replica", "tensor"),
        P("replica", "tensor"),
        P("replica", "tensor"),
        P("replica", "tensor"),
        P("replica", None),
        P("replica", None),
        P("replica"),
        P("replica"),
        P("replica"),
        P("replica"),
    )
    out_specs = (P(("replica", "tensor"), None), P("replica", "tensor"), P("replica", "tensor"))
    return jax.shard_map(
        per_device, mesh=mesh, in_specs=in_specs, out_specs=out_specs, check_vma=False
    )
```

```python
import functools
import math

import jax
import jax.numpy as jnp
from jax import lax
from jax.experimental import pallas as pl
from jax.experimental.pallas import tpu as pltpu
from jax.sharding import PartitionSpec as P

Q_HEADS = 64
KV_HEADS = 8
D_HEAD = 128
PAGE = 128
GROUP = Q_HEADS // KV_HEADS
SCALE = math.log2(math.e) / math.sqrt(D_HEAD)
LOW = -1e30
CHUNK = 512
VMEM_LIMIT = 60 * 2**20

NT = (((1,), (1,)), ((), ()))


def chunks_of(earlier, tail):
    starts = list(range(0, earlier, CHUNK)) + [earlier]
    return [(a, b - a) for a, b in zip(starts, starts[1:] + [earlier + tail])]


def prefill_kernel(
    tail, blk_ref, pages_ref, q_ref, k_hbm, v_hbm, o_ref,
    kbuf, vbuf, score_a, score_b, top_a, top_b, sem, *, first, pack, ones
):
    heads = kbuf.shape[0]
    count = pages_ref.shape[0]
    span = count * PAGE
    rows = q_ref.shape[0]
    units = GROUP // pack
    pieces = chunks_of(span - tail, tail)

    def fetch(head):
        cols = pl.ds(pl.multiple_of((first + head) * D_HEAD, D_HEAD), D_HEAD)

        def one(j, _):
            src = pl.ds(pl.multiple_of(pages_ref[j] * PAGE, PAGE), PAGE)
            dst = pl.ds(pl.multiple_of(j * PAGE, PAGE), PAGE)
            pltpu.make_async_copy(k_hbm.at[src, cols], kbuf.at[head, dst], sem.at[head, 0]).start()
            pltpu.make_async_copy(v_hbm.at[src, cols], vbuf.at[head, dst], sem.at[head, 1]).start()
            return 0

        lax.fori_loop(0, count, one, 0)

    def keys_ready(head):
        pltpu.make_async_copy(kbuf.at[head], kbuf.at[head], sem.at[head, 0]).wait()

    def values_ready(head):
        pltpu.make_async_copy(vbuf.at[head], vbuf.at[head], sem.at[head, 1]).wait()

    def columns(unit, h):
        return pl.ds(pl.multiple_of((unit * pack + h) * D_HEAD, D_HEAD), D_HEAD)

    def across(x, size):
        return jnp.concatenate([x] * (size // D_HEAD), axis=1)

    def run(now, later):
        if later is not None:
            unit, score, top = later
            head = unit // units
            q = jnp.concatenate([q_ref[:, columns(unit, h)] for h in range(pack)], axis=0)
            best = None
        if now is not None:
            unit_now, score_now, top_now = now
            head_now = unit_now // units
            shift = top_now[...]
            acc, total = None, None
        for start, size in pieces:
            if later is not None:
                keys = kbuf[head, start:start + size, :]
                s = lax.dot_general(q, keys, NT, preferred_element_type=jnp.float32)
                if start >= span - tail:
                    usable = lax.broadcasted_iota(jnp.int32, (rows, size), 1) <= (
                        lax.broadcasted_iota(jnp.int32, (rows, size), 0) + blk_ref[0] * rows
                    )
                    s = jnp.where(usable[None], s.reshape(pack, rows, size), LOW).reshape(s.shape)
                score[:, start:start + size] = s
                for at in range(0, size, D_HEAD):
                    piece = s[:, at:at + D_HEAD]
                    best = piece if best is None else jnp.maximum(best, piece)
            if now is not None:
                p = jnp.exp2(score_now[:, start:start + size] * SCALE - across(shift, size))
                values = vbuf[head_now, start:start + size, :]
                if ones:
                    values = jnp.concatenate([values, jnp.ones_like(values)], axis=1)
                else:
                    for at in range(0, size, D_HEAD):
                        piece = p[:, at:at + D_HEAD]
                        total = piece if total is None else total + piece
                o = jnp.dot(p.astype(jnp.bfloat16), values, preferred_element_type=jnp.float32)
                acc = o if acc is None else acc + o
        if later is not None:
            top[...] = jnp.broadcast_to(jnp.max(best, axis=1, keepdims=True) * SCALE, top.shape)
        if now is not None:
            total = acc[:, D_HEAD:] if ones else jnp.sum(total, axis=1, keepdims=True)
            o = (acc[:, :D_HEAD] / total).astype(o_ref.dtype)
            for h in range(pack):
                o_ref[:, columns(unit_now, h)] = o[h * rows:(h + 1) * rows]

    fetch(0)
    if heads > 1:
        fetch(1)
    keys_ready(0)
    a, b = (score_a, top_a), (score_b, top_b)
    run(None, (0, *a))
    values_ready(0)

    def body(i, _):
        u = 2 * i
        run((u, *a), (u + 1, *b))
        if heads > 1:
            head = (u + 2) // units

            @pl.when((u + 2) % units == 0)
            def _():
                @pl.when(head + 1 < heads)
                def _():
                    fetch(head + 1)

                keys_ready(head)
                values_ready(head)

        run((u + 1, *b), (u + 2, *a))
        return 0

    last = heads * units
    lax.fori_loop(0, last // 2 - 1, body, 0)
    run((last - 2, *a), (last - 1, *b))
    run((last - 1, *b), None)


def prefill_part(q, keys, values, pages, blk, ranks, first, heads, pack, ones, wide=False):
    tokens = q.shape[0]
    rows = tokens // ranks
    span = pages.shape[0] * PAGE
    width = heads * GROUP * D_HEAD
    total = ranks * keys.shape[1] // D_HEAD // heads if wide else 1
    work = heads * GROUP * rows * span

    return pl.pallas_call(
        functools.partial(prefill_kernel, tokens, first=first, pack=pack, ones=ones),
        grid_spec=pltpu.PrefetchScalarGridSpec(
            num_scalar_prefetch=2,
            grid=(1,),
            in_specs=[
                pl.BlockSpec((rows, width), lambda i, blk, pages: (blk[0], first // heads)),
                pl.BlockSpec(memory_space=pl.ANY),
                pl.BlockSpec(memory_space=pl.ANY),
            ],
            out_specs=pl.BlockSpec((rows, width), lambda i, blk, pages: (0, blk[0] if wide else 0)),
            scratch_shapes=[
                pltpu.VMEM((heads, span, D_HEAD), jnp.bfloat16),
                pltpu.VMEM((heads, span, D_HEAD), jnp.bfloat16),
                pltpu.VMEM((pack * rows, span), jnp.float32),
                pltpu.VMEM((pack * rows, span), jnp.float32),
                pltpu.VMEM((pack * rows, D_HEAD), jnp.float32),
                pltpu.VMEM((pack * rows, D_HEAD), jnp.float32),
                pltpu.SemaphoreType.DMA((heads, 2)),
            ],
        ),
        out_shape=jax.ShapeDtypeStruct((rows, total * width), q.dtype),
        compiler_params=pltpu.CompilerParams(vmem_limit_bytes=VMEM_LIMIT),
        cost_estimate=pl.CostEstimate(
            flops=4 * work * D_HEAD,
            bytes_accessed=4 * (heads * span * D_HEAD + rows * width),
            transcendentals=work,
        ),
        name="prefill",
    )(blk, pages, q, keys, values)


def small_kernel(
    over_pages, dec_pages, over_len, dec_len, dest_ref, over_ref, decq_ref, k_hbm, v_hbm,
    dec_ref, out_ref, kbuf, vbuf, q_all, res, flat, sem
):
    over, (dec, per) = over_pages.shape[0], dec_pages.shape
    count = over + dec * per
    batch = q_all.shape[0]
    keys = count * PAGE
    heads = q_all.shape[1] // D_HEAD

    for j in range(count):
        page = over_pages[j] if j < over else dec_pages[(j - over) // per, (j - over) % per]
        src = pl.ds(pl.multiple_of(page * PAGE, PAGE), PAGE)
        dst = pl.ds(j * PAGE, PAGE)
        pltpu.make_async_copy(k_hbm.at[src], kbuf.at[dst], sem.at[0]).start()
        pltpu.make_async_copy(v_hbm.at[src], vbuf.at[dst], sem.at[1]).start()

    if batch > over + dec:
        q_all[...] = jnp.zeros_like(q_all)
    q_all[0:over, :] = over_ref[...].astype(jnp.float32)
    q_all[over:over + dec, :] = decq_ref[...].astype(jnp.float32)
    out_ref[...] = jnp.zeros_like(out_ref)
    row = lax.broadcasted_iota(jnp.int32, (batch, PAGE), 0)
    lane = lax.broadcasted_iota(jnp.int32, (batch, PAGE), 1)
    masks = []
    for j in range(count):
        owner, base = (j, 0) if j < over else (over + (j - over) // per, (j - over) % per * PAGE)
        most = over_len[j] if j < over else dec_len[owner - over]
        masks.append((row == owner) & (lane + base < most))
    pltpu.make_async_copy(kbuf, kbuf, sem.at[0]).wait()
    for g in range(k_hbm.shape[1] // D_HEAD):
        cols = slice(g * D_HEAD, (g + 1) * D_HEAD)
        q = jnp.concatenate(
            [q_all[:, (g * GROUP + h) * D_HEAD:(g * GROUP + h + 1) * D_HEAD] for h in range(GROUP)],
            axis=0,
        ).astype(jnp.bfloat16)
        s = lax.dot_general(q, kbuf[:, cols], NT, preferred_element_type=jnp.float32)
        s = s.reshape(GROUP, batch, keys)
        s = jnp.concatenate(
            [
                jnp.where(masks[j][None], s[:, :, j * PAGE:(j + 1) * PAGE], LOW)
                for j in range(count)
            ],
            axis=2,
        ).reshape(GROUP * batch, keys)
        p = jnp.exp2((s - jnp.max(s, axis=1, keepdims=True)) * SCALE)
        total = jnp.sum(p, axis=1, keepdims=True)
        w = (p / total).astype(jnp.bfloat16)
        if g == 0:
            pltpu.make_async_copy(vbuf, vbuf, sem.at[1]).wait()
        o = jnp.dot(w, vbuf[:, cols], preferred_element_type=jnp.float32)
        for h in range(GROUP):
            at = g * GROUP + h
            res[:, at * D_HEAD:(at + 1) * D_HEAD] = o[h * batch:(h + 1) * batch]
            flat[pl.ds(at, batch, stride=heads), :] = o[h * batch:(h + 1) * batch]
    dec_ref[...] = res[over:over + dec, :].astype(dec_ref.dtype)
    for m in range(over):
        out_ref[dest_ref[m]] = flat[m * heads:(m + 1) * heads, :].astype(out_ref.dtype)


def small_part(decode_q, overflow_q, keys, values, dec_pages, over_pages, dec_len, over_len, dest, replicas):
    dec, over = decode_q.shape[0], overflow_q.shape[0]
    batch = -(-(dec + over) // 8) * 8
    width = decode_q.shape[1]
    span = (over + dec_pages.size) * PAGE
    work = batch * width * span
    moved = (replicas, width // D_HEAD, D_HEAD)
    return pl.pallas_call(
        small_kernel,
        grid_spec=pltpu.PrefetchScalarGridSpec(
            num_scalar_prefetch=5,
            grid=(1,),
            in_specs=[
                pl.BlockSpec((over, width), lambda i, *_: (0, 0)),
                pl.BlockSpec((dec, width), lambda i, *_: (0, 0)),
                pl.BlockSpec(memory_space=pl.ANY),
                pl.BlockSpec(memory_space=pl.ANY),
            ],
            out_specs=[
                pl.BlockSpec((dec, width), lambda i, *_: (0, 0)),
                pl.BlockSpec(moved, lambda i, *_: (0, 0, 0)),
            ],
            scratch_shapes=[
                pltpu.VMEM((span, keys.shape[1]), jnp.bfloat16),
                pltpu.VMEM((span, keys.shape[1]), jnp.bfloat16),
                pltpu.VMEM((batch, width), jnp.float32),
                pltpu.VMEM((batch, width), jnp.float32),
                pltpu.VMEM((batch * width // D_HEAD, D_HEAD), jnp.float32),
                pltpu.SemaphoreType.DMA((2,)),
            ],
        ),
        out_shape=[
            jax.ShapeDtypeStruct((dec, width), decode_q.dtype),
            jax.ShapeDtypeStruct(moved, decode_q.dtype),
        ],
        compiler_params=pltpu.CompilerParams(vmem_limit_bytes=VMEM_LIMIT),
        cost_estimate=pl.CostEstimate(
            flops=4 * work, bytes_accessed=4 * span * keys.shape[1], transcendentals=work // D_HEAD
        ),
        name="small",
    )(over_pages, dec_pages, over_len, dec_len, dest, overflow_q, decode_q, keys, values)


def finish_kernel(ranks, rank_ref, rows_ref, big_ref, *refs):
    got, (out_ref, mov_ref, flat, sem) = refs[:-4], refs[-4:]
    del big_ref
    cols = got[0].shape[1]
    heads = len(got) // (ranks - 1)
    copies = []
    for i, part in enumerate(got):
        source = lax.rem(rank_ref[0] + ranks - (i // heads + 1), ranks)
        to = pl.ds(pl.multiple_of((source * heads + i % heads) * cols, cols), cols)
        copies.append(pltpu.make_async_copy(part, out_ref.at[:, to], sem.at[i]))
        copies[-1].start()
    replicas, count, _ = rows_ref.shape
    flat[...] = rows_ref[...].astype(jnp.float32).reshape(flat.shape)
    for h in range(count):
        line = flat[pl.ds(h, replicas, stride=count), :]
        mov_ref[:, h * D_HEAD:(h + 1) * D_HEAD] = line.astype(mov_ref.dtype)
    for copy in copies:
        copy.wait()


def finish_part(rank, ranks, rows, big, got):
    replicas, count, _ = rows.shape
    anywhere = pl.BlockSpec(memory_space=pl.ANY)
    return pl.pallas_call(
        functools.partial(finish_kernel, ranks),
        grid_spec=pltpu.PrefetchScalarGridSpec(
            num_scalar_prefetch=1,
            grid=(1,),
            in_specs=[pl.BlockSpec(rows.shape, lambda i, *_: (0, 0, 0)), anywhere]
            + [pl.BlockSpec(memory_space=pltpu.VMEM)] * len(got),
            out_specs=[anywhere, pl.BlockSpec((replicas, count * D_HEAD), lambda i, *_: (0, 0))],
            scratch_shapes=[
                pltpu.VMEM((replicas * count, D_HEAD), jnp.float32),
                pltpu.SemaphoreType.DMA((len(got),)),
            ],
        ),
        out_shape=[
            jax.ShapeDtypeStruct(big.shape, big.dtype),
            jax.ShapeDtypeStruct((replicas, count * D_HEAD), big.dtype),
        ],
        input_output_aliases={2: 0},
        compiler_params=pltpu.CompilerParams(vmem_limit_bytes=VMEM_LIMIT),
        cost_estimate=pl.CostEstimate(
            flops=0, bytes_accessed=2 * big.size + 4 * rows.size, transcendentals=0
        ),
        name="finish",
    )(rank, rows, big, *got)


def per_device(
    prefill_q,
    decode_q,
    overflow_q,
    key_pool,
    value_pool,
    prefill_pages,
    decode_pages,
    decode_len,
    overflow_pages,
    overflow_len,
    overflow_dest,
):
    ranks, replicas = lax.axis_size("tensor"), lax.axis_size("replica")
    rank = lax.axis_index("tensor")
    heads = key_pool.shape[1] // D_HEAD
    pages = prefill_pages[0]

    decode_out, sent = small_part(
        decode_q,
        overflow_q,
        key_pool,
        value_pool,
        decode_pages,
        overflow_pages,
        decode_len,
        overflow_len,
        overflow_dest,
        replicas,
    )
    rows = lax.all_to_all(sent, "replica", split_axis=0, concat_axis=0, tiled=True)

    got = []
    for shift in range(1, ranks):
        blk = lax.rem(rank + shift, ranks)[None].astype(jnp.int32)
        step = min(heads, 2)
        for g in range(0, heads, step):
            part = prefill_part(
                prefill_q, key_pool, value_pool, pages, blk, ranks, g, step, pack=4, ones=True
            )
            got.append(lax.ppermute(part, "tensor", [(i, (i + shift) % ranks) for i in range(ranks)]))
    own = rank[None].astype(jnp.int32)
    prefill_out = prefill_part(
        prefill_q, key_pool, value_pool, pages, own, ranks, 0, heads, pack=4, ones=False, wide=True
    )
    prefill_out, moved_out = finish_part(own, ranks, rows, prefill_out, got)
    return (prefill_out, decode_out, moved_out)


def solution(mesh):
    in_specs = (
        P("replica", "tensor"),
        P("replica", "tensor"),
        P("replica", "tensor"),
        P("replica", "tensor"),
        P("replica", "tensor"),
        P("replica", None),
        P("replica", None),
        P("replica"),
        P("replica"),
        P("replica"),
        P("replica"),
    )
    out_specs = (P(("replica", "tensor"), None), P("replica", "tensor"), P("replica", "tensor"))
    return jax.shard_map(
        per_device, mesh=mesh, in_specs=in_specs, out_specs=out_specs, check_vma=False
    )
```

```python
import functools
import math

import jax
import jax.numpy as jnp
from jax import lax
from jax.experimental import pallas as pl
from jax.experimental.pallas import tpu as pltpu
from jax.sharding import PartitionSpec as P

Q_HEADS = 64
KV_HEADS = 8
D_HEAD = 128
PAGE = 128
GROUP = Q_HEADS // KV_HEADS
SCALE = math.log2(math.e) / math.sqrt(D_HEAD)
LOW = -1e30
CHUNK = 512
SLAB = 64
VMEM_LIMIT = 60 * 2**20

NT = (((1,), (1,)), ((), ()))


def chunks_of(earlier, tail):
    starts = list(range(0, earlier, CHUNK)) + [earlier]
    return [(a, b - a) for a, b in zip(starts, starts[1:] + [earlier + tail])]


def prefill_kernel(
    tail, blk_ref, pages_ref, q_ref, k_hbm, v_hbm, o_ref,
    kbuf, vbuf, score_a, score_b, top_a, top_b, sem, *, first, pack
):
    heads = kbuf.shape[0]
    count = pages_ref.shape[0]
    span = count * PAGE
    rows = q_ref.shape[0]
    units = GROUP // pack
    pieces = chunks_of(span - tail, tail)

    def fetch(head):
        cols = pl.ds(pl.multiple_of((first + head) * D_HEAD, D_HEAD), D_HEAD)

        def one(j, _):
            src = pl.ds(pl.multiple_of(pages_ref[j] * PAGE, PAGE), PAGE)
            dst = pl.ds(pl.multiple_of(j * PAGE, PAGE), PAGE)
            pltpu.make_async_copy(k_hbm.at[src, cols], kbuf.at[head, dst], sem.at[head, 0]).start()
            pltpu.make_async_copy(v_hbm.at[src, cols], vbuf.at[head, dst], sem.at[head, 1]).start()
            return 0

        lax.fori_loop(0, count, one, 0)

    def keys_ready(head):
        pltpu.make_async_copy(kbuf.at[head], kbuf.at[head], sem.at[head, 0]).wait()

    def values_ready(head):
        pltpu.make_async_copy(vbuf.at[head], vbuf.at[head], sem.at[head, 1]).wait()

    def columns(unit, h):
        return pl.ds(pl.multiple_of((unit * pack + h) * D_HEAD, D_HEAD), D_HEAD)

    def across(x, size):
        return jnp.concatenate([x] * (size // D_HEAD), axis=1)

    def fold(op, kept, x):
        for at in range(0, x.shape[1], D_HEAD):
            piece = x[:, at:at + D_HEAD]
            kept = piece if kept is None else op(kept, piece)
        return kept

    def run(now, later):
        if later is not None:
            unit, score, top = later
            head = unit // units
            q = jnp.concatenate([q_ref[:, columns(unit, h)] for h in range(pack)], axis=0)
        if now is not None:
            unit_now, score_now, top_now = now
            head_now = unit_now // units
        slabs = [(r, min(SLAB, pack * rows - r)) for r in range(0, pack * rows, SLAB)]
        best, total = [None] * len(slabs), [None] * len(slabs)
        acc = None
        for start, size in pieces:
            if later is not None:
                keys = kbuf[head, start:start + size, :]
                s = lax.dot_general(q, keys, NT, preferred_element_type=jnp.float32)
                if start >= span - tail:
                    usable = lax.broadcasted_iota(jnp.int32, (rows, size), 1) <= (
                        lax.broadcasted_iota(jnp.int32, (rows, size), 0) + blk_ref[0] * rows
                    )
                    s = jnp.where(usable[None], s.reshape(pack, rows, size), LOW).reshape(s.shape)
            weights = []
            for i, (r, n) in enumerate(slabs):
                if later is not None:
                    part = s[r:r + n]
                    score[r:r + n, start:start + size] = part
                    best[i] = fold(jnp.maximum, best[i], part)
                if now is not None:
                    x = score_now[r:r + n, start:start + size]
                    p = jnp.exp2(x * SCALE - across(top_now[r:r + n, :], size))
                    total[i] = fold(jnp.add, total[i], p)
                    weights.append(p.astype(jnp.bfloat16))
            if now is not None:
                values = vbuf[head_now, start:start + size, :]
                weights = jnp.concatenate(weights, axis=0)
                o = jnp.dot(weights, values, preferred_element_type=jnp.float32)
                acc = o if acc is None else acc + o
        if later is not None:
            for (r, n), peak in zip(slabs, best):
                peak = jnp.max(peak, axis=1, keepdims=True) * SCALE
                top[r:r + n, :] = jnp.broadcast_to(peak, (n, D_HEAD))
        if now is not None:
            total = jnp.concatenate([jnp.sum(t, axis=1, keepdims=True) for t in total], axis=0)
            o = (acc / total).astype(o_ref.dtype)
            for h in range(pack):
                o_ref[:, columns(unit_now, h)] = o[h * rows:(h + 1) * rows]

    fetch(0)
    if heads > 1:
        fetch(1)
    keys_ready(0)
    a, b = (score_a, top_a), (score_b, top_b)
    run(None, (0, *a))
    values_ready(0)

    def body(i, _):
        u = 2 * i
        run((u, *a), (u + 1, *b))
        if heads > 1:
            head = (u + 2) // units

            @pl.when((u + 2) % units == 0)
            def _():
                @pl.when(head + 1 < heads)
                def _():
                    fetch(head + 1)

                keys_ready(head)
                values_ready(head)

        run((u + 1, *b), (u + 2, *a))
        return 0

    last = heads * units
    lax.fori_loop(0, last // 2 - 1, body, 0)
    run((last - 2, *a), (last - 1, *b))
    run((last - 1, *b), None)


def prefill_part(q, keys, values, pages, blk, ranks, first, heads, pack, wide=False):
    tokens = q.shape[0]
    rows = tokens // ranks
    span = pages.shape[0] * PAGE
    width = heads * GROUP * D_HEAD
    total = ranks * keys.shape[1] // D_HEAD // heads if wide else 1
    work = heads * GROUP * rows * span

    return pl.pallas_call(
        functools.partial(prefill_kernel, tokens, first=first, pack=pack),
        grid_spec=pltpu.PrefetchScalarGridSpec(
            num_scalar_prefetch=2,
            grid=(1,),
            in_specs=[
                pl.BlockSpec((rows, width), lambda i, blk, pages: (blk[0], first // heads)),
                pl.BlockSpec(memory_space=pl.ANY),
                pl.BlockSpec(memory_space=pl.ANY),
            ],
            out_specs=pl.BlockSpec((rows, width), lambda i, blk, pages: (0, blk[0] if wide else 0)),
            scratch_shapes=[
                pltpu.VMEM((heads, span, D_HEAD), jnp.bfloat16),
                pltpu.VMEM((heads, span, D_HEAD), jnp.bfloat16),
                pltpu.VMEM((pack * rows, span), jnp.float32),
                pltpu.VMEM((pack * rows, span), jnp.float32),
                pltpu.VMEM((pack * rows, D_HEAD), jnp.float32),
                pltpu.VMEM((pack * rows, D_HEAD), jnp.float32),
                pltpu.SemaphoreType.DMA((heads, 2)),
            ],
        ),
        out_shape=jax.ShapeDtypeStruct((rows, total * width), q.dtype),
        compiler_params=pltpu.CompilerParams(vmem_limit_bytes=VMEM_LIMIT),
        cost_estimate=pl.CostEstimate(
            flops=4 * work * D_HEAD,
            bytes_accessed=4 * (heads * span * D_HEAD + rows * width),
            transcendentals=work,
        ),
        name="prefill",
    )(blk, pages, q, keys, values)


def small_kernel(
    over_pages, dec_pages, over_len, dec_len, dest_ref, over_ref, decq_ref, k_hbm, v_hbm,
    dec_ref, out_ref, kbuf, vbuf, q_all, res, flat, sem
):
    over, (dec, per) = over_pages.shape[0], dec_pages.shape
    count = over + dec * per
    batch = q_all.shape[0]
    keys = count * PAGE
    heads = q_all.shape[1] // D_HEAD

    for j in range(count):
        page = over_pages[j] if j < over else dec_pages[(j - over) // per, (j - over) % per]
        src = pl.ds(pl.multiple_of(page * PAGE, PAGE), PAGE)
        dst = pl.ds(j * PAGE, PAGE)
        pltpu.make_async_copy(k_hbm.at[src], kbuf.at[dst], sem.at[0]).start()
        pltpu.make_async_copy(v_hbm.at[src], vbuf.at[dst], sem.at[1]).start()

    if batch > over + dec:
        q_all[...] = jnp.zeros_like(q_all)
    q_all[0:over, :] = over_ref[...].astype(jnp.float32)
    q_all[over:over + dec, :] = decq_ref[...].astype(jnp.float32)
    out_ref[...] = jnp.zeros_like(out_ref)
    row = lax.broadcasted_iota(jnp.int32, (batch, PAGE), 0)
    lane = lax.broadcasted_iota(jnp.int32, (batch, PAGE), 1)
    masks = []
    for j in range(count):
        owner, base = (j, 0) if j < over else (over + (j - over) // per, (j - over) % per * PAGE)
        most = over_len[j] if j < over else dec_len[owner - over]
        masks.append((row == owner) & (lane + base < most))
    pltpu.make_async_copy(kbuf, kbuf, sem.at[0]).wait()
    for g in range(k_hbm.shape[1] // D_HEAD):
        cols = slice(g * D_HEAD, (g + 1) * D_HEAD)
        q = jnp.concatenate(
            [q_all[:, (g * GROUP + h) * D_HEAD:(g * GROUP + h + 1) * D_HEAD] for h in range(GROUP)],
            axis=0,
        ).astype(jnp.bfloat16)
        s = lax.dot_general(q, kbuf[:, cols], NT, preferred_element_type=jnp.float32)
        s = s.reshape(GROUP, batch, keys)
        s = jnp.concatenate(
            [
                jnp.where(masks[j][None], s[:, :, j * PAGE:(j + 1) * PAGE], LOW)
                for j in range(count)
            ],
            axis=2,
        ).reshape(GROUP * batch, keys)
        p = jnp.exp2((s - jnp.max(s, axis=1, keepdims=True)) * SCALE)
        total = jnp.sum(p, axis=1, keepdims=True)
        w = (p / total).astype(jnp.bfloat16)
        if g == 0:
            pltpu.make_async_copy(vbuf, vbuf, sem.at[1]).wait()
        o = jnp.dot(w, vbuf[:, cols], preferred_element_type=jnp.float32)
        for h in range(GROUP):
            at = g * GROUP + h
            res[:, at * D_HEAD:(at + 1) * D_HEAD] = o[h * batch:(h + 1) * batch]
            flat[pl.ds(at, batch, stride=heads), :] = o[h * batch:(h + 1) * batch]
    dec_ref[...] = res[over:over + dec, :].astype(dec_ref.dtype)
    for m in range(over):
        out_ref[dest_ref[m]] = flat[m * heads:(m + 1) * heads, :].astype(out_ref.dtype)


def small_part(decode_q, overflow_q, keys, values, dec_pages, over_pages, dec_len, over_len, dest, replicas):
    dec, over = decode_q.shape[0], overflow_q.shape[0]
    batch = -(-(dec + over) // 8) * 8
    width = decode_q.shape[1]
    span = (over + dec_pages.size) * PAGE
    work = batch * width * span
    moved = (replicas, width // D_HEAD, D_HEAD)
    return pl.pallas_call(
        small_kernel,
        grid_spec=pltpu.PrefetchScalarGridSpec(
            num_scalar_prefetch=5,
            grid=(1,),
            in_specs=[
                pl.BlockSpec((over, width), lambda i, *_: (0, 0)),
                pl.BlockSpec((dec, width), lambda i, *_: (0, 0)),
                pl.BlockSpec(memory_space=pl.ANY),
                pl.BlockSpec(memory_space=pl.ANY),
            ],
            out_specs=[
                pl.BlockSpec((dec, width), lambda i, *_: (0, 0)),
                pl.BlockSpec(moved, lambda i, *_: (0, 0, 0)),
            ],
            scratch_shapes=[
                pltpu.VMEM((span, keys.shape[1]), jnp.bfloat16),
                pltpu.VMEM((span, keys.shape[1]), jnp.bfloat16),
                pltpu.VMEM((batch, width), jnp.float32),
                pltpu.VMEM((batch, width), jnp.float32),
                pltpu.VMEM((batch * width // D_HEAD, D_HEAD), jnp.float32),
                pltpu.SemaphoreType.DMA((2,)),
            ],
        ),
        out_shape=[
            jax.ShapeDtypeStruct((dec, width), decode_q.dtype),
            jax.ShapeDtypeStruct(moved, decode_q.dtype),
        ],
        compiler_params=pltpu.CompilerParams(vmem_limit_bytes=VMEM_LIMIT),
        cost_estimate=pl.CostEstimate(
            flops=4 * work, bytes_accessed=4 * span * keys.shape[1], transcendentals=work // D_HEAD
        ),
        name="small",
    )(over_pages, dec_pages, over_len, dec_len, dest, overflow_q, decode_q, keys, values)


def finish_kernel(ranks, rank_ref, rows_ref, big_ref, *refs):
    got, (out_ref, mov_ref, flat, sem) = refs[:-4], refs[-4:]
    del big_ref
    cols = got[0].shape[1]
    heads = len(got) // (ranks - 1)
    copies = []
    for i, part in enumerate(got):
        source = lax.rem(rank_ref[0] + ranks - (i // heads + 1), ranks)
        to = pl.ds(pl.multiple_of((source * heads + i % heads) * cols, cols), cols)
        copies.append(pltpu.make_async_copy(part, out_ref.at[:, to], sem.at[i]))
        copies[-1].start()
    replicas, count, _ = rows_ref.shape
    flat[...] = rows_ref[...].astype(jnp.float32).reshape(flat.shape)
    for h in range(count):
        line = flat[pl.ds(h, replicas, stride=count), :]
        mov_ref[:, h * D_HEAD:(h + 1) * D_HEAD] = line.astype(mov_ref.dtype)
    for copy in copies:
        copy.wait()


def finish_part(rank, ranks, rows, big, got):
    replicas, count, _ = rows.shape
    anywhere = pl.BlockSpec(memory_space=pl.ANY)
    return pl.pallas_call(
        functools.partial(finish_kernel, ranks),
        grid_spec=pltpu.PrefetchScalarGridSpec(
            num_scalar_prefetch=1,
            grid=(1,),
            in_specs=[pl.BlockSpec(rows.shape, lambda i, *_: (0, 0, 0)), anywhere]
            + [pl.BlockSpec(memory_space=pltpu.VMEM)] * len(got),
            out_specs=[anywhere, pl.BlockSpec((replicas, count * D_HEAD), lambda i, *_: (0, 0))],
            scratch_shapes=[
                pltpu.VMEM((replicas * count, D_HEAD), jnp.float32),
                pltpu.SemaphoreType.DMA((len(got),)),
            ],
        ),
        out_shape=[
            jax.ShapeDtypeStruct(big.shape, big.dtype),
            jax.ShapeDtypeStruct((replicas, count * D_HEAD), big.dtype),
        ],
        input_output_aliases={2: 0},
        compiler_params=pltpu.CompilerParams(vmem_limit_bytes=16 * 2**20),
        cost_estimate=pl.CostEstimate(
            flops=0, bytes_accessed=2 * big.size + 4 * rows.size, transcendentals=0
        ),
        name="finish",
    )(rank, rows, big, *got)


def per_device(
    prefill_q,
    decode_q,
    overflow_q,
    key_pool,
    value_pool,
    prefill_pages,
    decode_pages,
    decode_len,
    overflow_pages,
    overflow_len,
    overflow_dest,
):
    ranks, replicas = lax.axis_size("tensor"), lax.axis_size("replica")
    rank = lax.axis_index("tensor")
    heads = key_pool.shape[1] // D_HEAD
    pages = prefill_pages[0]

    decode_out, sent = small_part(
        decode_q,
        overflow_q,
        key_pool,
        value_pool,
        decode_pages,
        overflow_pages,
        decode_len,
        overflow_len,
        overflow_dest,
        replicas,
    )
    sent, pages = lax.optimization_barrier((sent, pages))
    rows = lax.all_to_all(sent, "replica", split_axis=0, concat_axis=0, tiled=True)

    got = []
    for shift in range(1, ranks):
        blk = lax.rem(rank + shift, ranks)[None].astype(jnp.int32)
        step = min(heads, 2)
        for g in range(0, heads, step):
            part = prefill_part(
                prefill_q, key_pool, value_pool, pages, blk, ranks, g, step, pack=4
            )
            got.append(lax.ppermute(part, "tensor", [(i, (i + shift) % ranks) for i in range(ranks)]))
    own = rank[None].astype(jnp.int32)
    prefill_out = prefill_part(
        prefill_q, key_pool, value_pool, pages, own, ranks, 0, heads, pack=4, wide=True
    )
    prefill_out, moved_out = finish_part(own, ranks, rows, prefill_out, got)
    return (prefill_out, decode_out, moved_out)


def solution(mesh):
    in_specs = (
        P("replica", "tensor"),
        P("replica", "tensor"),
        P("replica", "tensor"),
        P("replica", "tensor"),
        P("replica", "tensor"),
        P("replica", None),
        P("replica", None),
        P("replica"),
        P("replica"),
        P("replica"),
        P("replica"),
    )
    out_specs = (P(("replica", "tensor"), None), P("replica", "tensor"), P("replica", "tensor"))
    return jax.shard_map(
        per_device, mesh=mesh, in_specs=in_specs, out_specs=out_specs, check_vma=False
    )
```

```python
import functools
import math

import jax
import jax.numpy as jnp
from jax import lax
from jax.experimental import pallas as pl
from jax.experimental.pallas import tpu as pltpu
from jax.sharding import PartitionSpec as P

Q_HEADS = 64
KV_HEADS = 8
D_HEAD = 128
PAGE = 128
GROUP = Q_HEADS // KV_HEADS
SCALE = math.log2(math.e) / math.sqrt(D_HEAD)
LOW = -1e30
CHUNK = 512
VMEM_LIMIT = 60 * 2**20

NT = (((1,), (1,)), ((), ()))


def chunks_of(earlier, tail):
    starts = list(range(0, earlier, CHUNK)) + [earlier]
    return [(a, b - a) for a, b in zip(starts, starts[1:] + [earlier + tail])]


def prefill_kernel(
    tail, blk_ref, pages_ref, q_ref, k_hbm, v_hbm, o_ref,
    kbuf, vbuf, score, top, acc, sem, *, first, pack
):
    heads = kbuf.shape[0]
    count = pages_ref.shape[0]
    span = count * PAGE
    rows = q_ref.shape[0]
    units = GROUP // pack
    pieces = chunks_of(span - tail, tail)

    def fetch(head):
        cols = pl.ds(pl.multiple_of((first + head) * D_HEAD, D_HEAD), D_HEAD)

        def one(j, _):
            src = pl.ds(pl.multiple_of(pages_ref[j] * PAGE, PAGE), PAGE)
            dst = pl.ds(pl.multiple_of(j * PAGE, PAGE), PAGE)
            pltpu.make_async_copy(k_hbm.at[src, cols], kbuf.at[head, dst], sem.at[head, 0]).start()
            pltpu.make_async_copy(v_hbm.at[src, cols], vbuf.at[head, dst], sem.at[head, 1]).start()
            return 0

        lax.fori_loop(0, count, one, 0)

    def keys_ready(head):
        pltpu.make_async_copy(kbuf.at[head], kbuf.at[head], sem.at[head, 0]).wait()

    def values_ready(head):
        pltpu.make_async_copy(vbuf.at[head], vbuf.at[head], sem.at[head, 1]).wait()

    def columns(unit, h):
        return pl.ds(pl.multiple_of((unit * pack + h) * D_HEAD, D_HEAD), D_HEAD)

    def across(x, size):
        return jnp.concatenate([x] * (size // D_HEAD), axis=1)

    def fold(op, kept, x):
        for at in range(0, x.shape[1], D_HEAD):
            piece = x[:, at:at + D_HEAD]
            kept = piece if kept is None else op(kept, piece)
        return kept

    def tops(u):
        return pl.when(u >= 0)

    def unit(u, _):
        head = u // units

        @pl.when((u % units == 0) & (head + 1 < heads))
        def _():
            fetch(head + 1)

        @pl.when(u % units == 0)
        def _():
            keys_ready(head)

        for i, (start, size) in enumerate(pieces):

            @tops(u)
            def _(i=i, start=start, size=size):
                q = jnp.concatenate([q_ref[:, columns(u, h)] for h in range(pack)], axis=0)
                keys = kbuf[head, start:start + size, :]
                s = lax.dot_general(q, keys, NT, preferred_element_type=jnp.float32)
                if start >= span - tail:
                    usable = lax.broadcasted_iota(jnp.int32, (rows, size), 1) <= (
                        lax.broadcasted_iota(jnp.int32, (rows, size), 0)
                        + (blk_ref[0] * rows + span - tail - start)
                    )
                    s = jnp.where(usable[None], s.reshape(pack, rows, size), LOW).reshape(s.shape)
                score[:, start:start + size] = s
                peak = fold(jnp.maximum, None, s)
                if i > 0:
                    peak = jnp.maximum(peak, top[...])
                if start + size == span:
                    peak = jnp.max(peak, axis=1, keepdims=True) * SCALE
                    peak = jnp.broadcast_to(peak, top.shape)
                top[...] = peak

        @pl.when(u % units == 0)
        def _():
            values_ready(head)

        for i, (start, size) in enumerate(pieces):

            @tops(u)
            def _(i=i, start=start, size=size):
                x = score[:, start:start + size]
                p = jnp.exp2(x * SCALE - across(top[...], size))
                values = vbuf[head, start:start + size, :]
                values = jnp.concatenate([values, jnp.ones_like(values)], axis=1)
                o = jnp.dot(p.astype(jnp.bfloat16), values, preferred_element_type=jnp.float32)
                if i > 0:
                    o = o + acc[...]
                if start + size < span:
                    acc[...] = o
                else:
                    o = (o[:, :D_HEAD] / o[:, D_HEAD:]).astype(o_ref.dtype)
                    for h in range(pack):
                        o_ref[:, columns(u, h)] = o[h * rows:(h + 1) * rows]

        return 0

    fetch(0)
    lax.fori_loop(0, heads * units, unit, 0)


def prefill_part(q, keys, values, pages, blk, ranks, first, heads, pack, wide=False):
    tokens = q.shape[0]
    rows = tokens // ranks
    span = pages.shape[0] * PAGE
    width = heads * GROUP * D_HEAD
    total = ranks * keys.shape[1] // D_HEAD // heads if wide else 1
    work = heads * GROUP * rows * span

    return pl.pallas_call(
        functools.partial(prefill_kernel, tokens, first=first, pack=pack),
        grid_spec=pltpu.PrefetchScalarGridSpec(
            num_scalar_prefetch=2,
            grid=(1,),
            in_specs=[
                pl.BlockSpec((rows, width), lambda i, blk, pages: (blk[0], first // heads)),
                pl.BlockSpec(memory_space=pl.ANY),
                pl.BlockSpec(memory_space=pl.ANY),
            ],
            out_specs=pl.BlockSpec((rows, width), lambda i, blk, pages: (0, blk[0] if wide else 0)),
            scratch_shapes=[
                pltpu.VMEM((heads, span, D_HEAD), jnp.bfloat16),
                pltpu.VMEM((heads, span, D_HEAD), jnp.bfloat16),
                pltpu.VMEM((pack * rows, span), jnp.float32),
                pltpu.VMEM((pack * rows, D_HEAD), jnp.float32),
                pltpu.VMEM((pack * rows, 2 * D_HEAD), jnp.float32),
                pltpu.SemaphoreType.DMA((heads, 2)),
            ],
        ),
        out_shape=jax.ShapeDtypeStruct((rows, total * width), q.dtype),
        compiler_params=pltpu.CompilerParams(vmem_limit_bytes=VMEM_LIMIT),
        cost_estimate=pl.CostEstimate(
            flops=4 * work * D_HEAD,
            bytes_accessed=4 * (heads * span * D_HEAD + rows * width),
            transcendentals=work,
        ),
        name="prefill",
    )(blk, pages, q, keys, values)


def small_kernel(
    over_pages, dec_pages, over_len, dec_len, dest_ref, over_ref, decq_ref, k_hbm, v_hbm,
    dec_ref, out_ref, kbuf, vbuf, q_all, res, flat, sem
):
    over, (dec, per) = over_pages.shape[0], dec_pages.shape
    count = over + dec * per
    batch = q_all.shape[0]
    keys = count * PAGE
    heads = q_all.shape[1] // D_HEAD

    for j in range(count):
        page = over_pages[j] if j < over else dec_pages[(j - over) // per, (j - over) % per]
        src = pl.ds(pl.multiple_of(page * PAGE, PAGE), PAGE)
        dst = pl.ds(j * PAGE, PAGE)
        pltpu.make_async_copy(k_hbm.at[src], kbuf.at[dst], sem.at[0]).start()
        pltpu.make_async_copy(v_hbm.at[src], vbuf.at[dst], sem.at[1]).start()

    if batch > over + dec:
        q_all[...] = jnp.zeros_like(q_all)
    q_all[0:over, :] = over_ref[...].astype(jnp.float32)
    q_all[over:over + dec, :] = decq_ref[...].astype(jnp.float32)
    out_ref[...] = jnp.zeros_like(out_ref)
    row = lax.broadcasted_iota(jnp.int32, (batch, PAGE), 0)
    lane = lax.broadcasted_iota(jnp.int32, (batch, PAGE), 1)
    masks = []
    for j in range(count):
        owner, base = (j, 0) if j < over else (over + (j - over) // per, (j - over) % per * PAGE)
        most = over_len[j] if j < over else dec_len[owner - over]
        masks.append((row == owner) & (lane + base < most))
    pltpu.make_async_copy(kbuf, kbuf, sem.at[0]).wait()
    for g in range(k_hbm.shape[1] // D_HEAD):
        cols = slice(g * D_HEAD, (g + 1) * D_HEAD)
        q = jnp.concatenate(
            [q_all[:, (g * GROUP + h) * D_HEAD:(g * GROUP + h + 1) * D_HEAD] for h in range(GROUP)],
            axis=0,
        ).astype(jnp.bfloat16)
        s = lax.dot_general(q, kbuf[:, cols], NT, preferred_element_type=jnp.float32)
        s = s.reshape(GROUP, batch, keys)
        s = jnp.concatenate(
            [
                jnp.where(masks[j][None], s[:, :, j * PAGE:(j + 1) * PAGE], LOW)
                for j in range(count)
            ],
            axis=2,
        ).reshape(GROUP * batch, keys)
        p = jnp.exp2((s - jnp.max(s, axis=1, keepdims=True)) * SCALE)
        total = jnp.sum(p, axis=1, keepdims=True)
        w = (p / total).astype(jnp.bfloat16)
        if g == 0:
            pltpu.make_async_copy(vbuf, vbuf, sem.at[1]).wait()
        o = jnp.dot(w, vbuf[:, cols], preferred_element_type=jnp.float32)
        for h in range(GROUP):
            at = g * GROUP + h
            res[:, at * D_HEAD:(at + 1) * D_HEAD] = o[h * batch:(h + 1) * batch]
            flat[pl.ds(at, batch, stride=heads), :] = o[h * batch:(h + 1) * batch]
    dec_ref[...] = res[over:over + dec, :].astype(dec_ref.dtype)
    for m in range(over):
        out_ref[dest_ref[m]] = flat[m * heads:(m + 1) * heads, :].astype(out_ref.dtype)


def small_part(decode_q, overflow_q, keys, values, dec_pages, over_pages, dec_len, over_len, dest, replicas):
    dec, over = decode_q.shape[0], overflow_q.shape[0]
    batch = -(-(dec + over) // 8) * 8
    width = decode_q.shape[1]
    span = (over + dec_pages.size) * PAGE
    work = batch * width * span
    moved = (replicas, width // D_HEAD, D_HEAD)
    return pl.pallas_call(
        small_kernel,
        grid_spec=pltpu.PrefetchScalarGridSpec(
            num_scalar_prefetch=5,
            grid=(1,),
            in_specs=[
                pl.BlockSpec((over, width), lambda i, *_: (0, 0)),
                pl.BlockSpec((dec, width), lambda i, *_: (0, 0)),
                pl.BlockSpec(memory_space=pl.ANY),
                pl.BlockSpec(memory_space=pl.ANY),
            ],
            out_specs=[
                pl.BlockSpec((dec, width), lambda i, *_: (0, 0)),
                pl.BlockSpec(moved, lambda i, *_: (0, 0, 0)),
            ],
            scratch_shapes=[
                pltpu.VMEM((span, keys.shape[1]), jnp.bfloat16),
                pltpu.VMEM((span, keys.shape[1]), jnp.bfloat16),
                pltpu.VMEM((batch, width), jnp.float32),
                pltpu.VMEM((batch, width), jnp.float32),
                pltpu.VMEM((batch * width // D_HEAD, D_HEAD), jnp.float32),
                pltpu.SemaphoreType.DMA((2,)),
            ],
        ),
        out_shape=[
            jax.ShapeDtypeStruct((dec, width), decode_q.dtype),
            jax.ShapeDtypeStruct(moved, decode_q.dtype),
        ],
        compiler_params=pltpu.CompilerParams(vmem_limit_bytes=VMEM_LIMIT),
        cost_estimate=pl.CostEstimate(
            flops=4 * work, bytes_accessed=4 * span * keys.shape[1], transcendentals=work // D_HEAD
        ),
        name="small",
    )(over_pages, dec_pages, over_len, dec_len, dest, overflow_q, decode_q, keys, values)


def finish_kernel(ranks, rank_ref, rows_ref, big_ref, *refs):
    got, (out_ref, mov_ref, flat, sem) = refs[:-4], refs[-4:]
    del big_ref
    cols = got[0].shape[1]
    heads = len(got) // (ranks - 1)
    copies = []
    for i, part in enumerate(got):
        source = lax.rem(rank_ref[0] + ranks - (i // heads + 1), ranks)
        to = pl.ds(pl.multiple_of((source * heads + i % heads) * cols, cols), cols)
        copies.append(pltpu.make_async_copy(part, out_ref.at[:, to], sem.at[i]))
        copies[-1].start()
    replicas, count, _ = rows_ref.shape
    flat[...] = rows_ref[...].astype(jnp.float32).reshape(flat.shape)
    for h in range(count):
        line = flat[pl.ds(h, replicas, stride=count), :]
        mov_ref[:, h * D_HEAD:(h + 1) * D_HEAD] = line.astype(mov_ref.dtype)
    for copy in copies:
        copy.wait()


def finish_part(rank, ranks, rows, big, got):
    replicas, count, _ = rows.shape
    anywhere = pl.BlockSpec(memory_space=pl.ANY)
    return pl.pallas_call(
        functools.partial(finish_kernel, ranks),
        grid_spec=pltpu.PrefetchScalarGridSpec(
            num_scalar_prefetch=1,
            grid=(1,),
            in_specs=[pl.BlockSpec(rows.shape, lambda i, *_: (0, 0, 0)), anywhere]
            + [pl.BlockSpec(memory_space=pltpu.VMEM)] * len(got),
            out_specs=[anywhere, pl.BlockSpec((replicas, count * D_HEAD), lambda i, *_: (0, 0))],
            scratch_shapes=[
                pltpu.VMEM((replicas * count, D_HEAD), jnp.float32),
                pltpu.SemaphoreType.DMA((len(got),)),
            ],
        ),
        out_shape=[
            jax.ShapeDtypeStruct(big.shape, big.dtype),
            jax.ShapeDtypeStruct((replicas, count * D_HEAD), big.dtype),
        ],
        input_output_aliases={2: 0},
        compiler_params=pltpu.CompilerParams(vmem_limit_bytes=16 * 2**20),
        cost_estimate=pl.CostEstimate(
            flops=0, bytes_accessed=2 * big.size + 4 * rows.size, transcendentals=0
        ),
        name="finish",
    )(rank, rows, big, *got)


def per_device(
    prefill_q,
    decode_q,
    overflow_q,
    key_pool,
    value_pool,
    prefill_pages,
    decode_pages,
    decode_len,
    overflow_pages,
    overflow_len,
    overflow_dest,
):
    ranks, replicas = lax.axis_size("tensor"), lax.axis_size("replica")
    rank = lax.axis_index("tensor")
    heads = key_pool.shape[1] // D_HEAD
    pages = prefill_pages[0]

    decode_out, sent = small_part(
        decode_q,
        overflow_q,
        key_pool,
        value_pool,
        decode_pages,
        overflow_pages,
        decode_len,
        overflow_len,
        overflow_dest,
        replicas,
    )
    sent, pages = lax.optimization_barrier((sent, pages))
    rows = lax.all_to_all(sent, "replica", split_axis=0, concat_axis=0, tiled=True)

    got = []
    for shift in range(1, ranks):
        blk = lax.rem(rank + shift, ranks)[None].astype(jnp.int32)
        step = min(heads, 2)
        for g in range(0, heads, step):
            part = prefill_part(
                prefill_q, key_pool, value_pool, pages, blk, ranks, g, step, pack=4
            )
            got.append(lax.ppermute(part, "tensor", [(i, (i + shift) % ranks) for i in range(ranks)]))
    own = rank[None].astype(jnp.int32)
    prefill_out = prefill_part(
        prefill_q, key_pool, value_pool, pages, own, ranks, 0, heads, pack=8, wide=True
    )
    prefill_out, moved_out = finish_part(own, ranks, rows, prefill_out, got)
    return (prefill_out, decode_out, moved_out)


def solution(mesh):
    in_specs = (
        P("replica", "tensor"),
        P("replica", "tensor"),
        P("replica", "tensor"),
        P("replica", "tensor"),
        P("replica", "tensor"),
        P("replica", None),
        P("replica", None),
        P("replica"),
        P("replica"),
        P("replica"),
        P("replica"),
    )
    out_specs = (P(("replica", "tensor"), None), P("replica", "tensor"), P("replica", "tensor"))
    return jax.shard_map(
        per_device, mesh=mesh, in_specs=in_specs, out_specs=out_specs, check_vma=False
    )
```

```python
import functools
import math

import jax
import jax.numpy as jnp
from jax import lax
from jax.experimental import pallas as pl
from jax.experimental.pallas import tpu as pltpu
from jax.sharding import PartitionSpec as P

Q_HEADS = 64
KV_HEADS = 8
D_HEAD = 128
PAGE = 128
GROUP = Q_HEADS // KV_HEADS
SCALE = math.log2(math.e) / math.sqrt(D_HEAD)
LOW = -1e30
CHUNK = 512
VMEM_LIMIT = 60 * 2**20

NT = (((1,), (1,)), ((), ()))


def chunks_of(earlier, tail):
    starts = list(range(0, earlier, CHUNK)) + [earlier]
    return [(a, b - a) for a, b in zip(starts, starts[1:] + [earlier + tail])]


def prefill_kernel(
    tail, blk_ref, pages_ref, q_ref, k_hbm, v_hbm, o_ref,
    kbuf, vbuf, score, top, acc, sem, *, first, pack
):
    heads = kbuf.shape[0]
    count = pages_ref.shape[0]
    span = count * PAGE
    rows = q_ref.shape[0]
    units = GROUP // pack
    pieces = chunks_of(span - tail, tail)

    def fetch(head):
        cols = pl.ds(pl.multiple_of((first + head) * D_HEAD, D_HEAD), D_HEAD)

        for kind, (pool, buf) in enumerate(((k_hbm, kbuf), (v_hbm, vbuf))):

            def one(j, _):
                src = pl.ds(pl.multiple_of(pages_ref[j] * PAGE, PAGE), PAGE)
                dst = pl.ds(pl.multiple_of(j * PAGE, PAGE), PAGE)
                pltpu.make_async_copy(
                    pool.at[src, cols], buf.at[head, dst], sem.at[head, kind]
                ).start()
                return 0

            lax.fori_loop(0, count, one, 0)

    def keys_ready(head):
        pltpu.make_async_copy(kbuf.at[head], kbuf.at[head], sem.at[head, 0]).wait()

    def values_ready(head):
        pltpu.make_async_copy(vbuf.at[head], vbuf.at[head], sem.at[head, 1]).wait()

    def columns(unit, h):
        return pl.ds(pl.multiple_of((unit * pack + h) * D_HEAD, D_HEAD), D_HEAD)

    def across(x, size):
        return jnp.concatenate([x] * (size // D_HEAD), axis=1)

    def fold(op, kept, x):
        for at in range(0, x.shape[1], D_HEAD):
            piece = x[:, at:at + D_HEAD]
            kept = piece if kept is None else op(kept, piece)
        return kept

    def tops(u):
        return pl.when(u >= 0)

    def unit(u, _):
        head = u // units

        @pl.when((u % units == 0) & (head + 1 < heads))
        def _():
            fetch(head + 1)

        @pl.when(u % units == 0)
        def _():
            keys_ready(head)

        for i, (start, size) in enumerate(pieces):

            @tops(u)
            def _(i=i, start=start, size=size):
                q = jnp.concatenate([q_ref[:, columns(u, h)] for h in range(pack)], axis=0)
                keys = kbuf[head, start:start + size, :]
                s = lax.dot_general(q, keys, NT, preferred_element_type=jnp.float32)
                if start >= span - tail:
                    usable = lax.broadcasted_iota(jnp.int32, (rows, size), 1) <= (
                        lax.broadcasted_iota(jnp.int32, (rows, size), 0)
                        + (blk_ref[0] * rows + span - tail - start)
                    )
                    s = jnp.where(usable[None], s.reshape(pack, rows, size), LOW).reshape(s.shape)
                score[:, start:start + size] = s
                peak = fold(jnp.maximum, None, s)
                if i > 0:
                    peak = jnp.maximum(peak, top[...])
                if start + size == span:
                    peak = jnp.max(peak, axis=1, keepdims=True) * SCALE
                    peak = jnp.broadcast_to(peak, top.shape)
                top[...] = peak

        @pl.when(u % units == 0)
        def _():
            values_ready(head)

        for i, (start, size) in enumerate(pieces):

            @tops(u)
            def _(i=i, start=start, size=size):
                x = score[:, start:start + size]
                p = jnp.exp2(x * SCALE - across(top[...], size))
                values = vbuf[head, start:start + size, :]
                values = jnp.concatenate([values, jnp.ones_like(values)], axis=1)
                o = jnp.dot(p.astype(jnp.bfloat16), values, preferred_element_type=jnp.float32)
                if i > 0:
                    o = o + acc[...]
                if start + size < span:
                    acc[...] = o
                else:
                    o = (o[:, :D_HEAD] / o[:, D_HEAD:]).astype(o_ref.dtype)
                    for h in range(pack):
                        o_ref[:, columns(u, h)] = o[h * rows:(h + 1) * rows]

        return 0

    fetch(0)
    lax.fori_loop(0, heads * units, unit, 0)


def prefill_part(q, keys, values, pages, blk, ranks, first, heads, pack, wide=False):
    tokens = q.shape[0]
    rows = tokens // ranks
    span = pages.shape[0] * PAGE
    width = heads * GROUP * D_HEAD
    total = ranks * keys.shape[1] // D_HEAD // heads if wide else 1
    work = heads * GROUP * rows * span

    return pl.pallas_call(
        functools.partial(prefill_kernel, tokens, first=first, pack=pack),
        grid_spec=pltpu.PrefetchScalarGridSpec(
            num_scalar_prefetch=2,
            grid=(1,),
            in_specs=[
                pl.BlockSpec((rows, width), lambda i, blk, pages: (blk[0], first // heads)),
                pl.BlockSpec(memory_space=pl.ANY),
                pl.BlockSpec(memory_space=pl.ANY),
            ],
            out_specs=pl.BlockSpec((rows, width), lambda i, blk, pages: (0, blk[0] if wide else 0)),
            scratch_shapes=[
                pltpu.VMEM((heads, span, D_HEAD), jnp.bfloat16),
                pltpu.VMEM((heads, span, D_HEAD), jnp.bfloat16),
                pltpu.VMEM((pack * rows, span), jnp.float32),
                pltpu.VMEM((pack * rows, D_HEAD), jnp.float32),
                pltpu.VMEM((pack * rows, 2 * D_HEAD), jnp.float32),
                pltpu.SemaphoreType.DMA((heads, 2)),
            ],
        ),
        out_shape=jax.ShapeDtypeStruct((rows, total * width), q.dtype),
        compiler_params=pltpu.CompilerParams(vmem_limit_bytes=VMEM_LIMIT),
        cost_estimate=pl.CostEstimate(
            flops=4 * work * D_HEAD,
            bytes_accessed=4 * (heads * span * D_HEAD + rows * width),
            transcendentals=work,
        ),
        name="prefill",
    )(blk, pages, q, keys, values)


def small_kernel(
    over_pages, dec_pages, over_len, dec_len, dest_ref, over_ref, decq_ref, k_hbm, v_hbm,
    dec_ref, out_ref, kbuf, vbuf, q_all, res, bias, flat, sem
):
    over, (dec, per) = over_pages.shape[0], dec_pages.shape
    count = over + dec * per
    batch = q_all.shape[0]
    keys = count * PAGE
    heads = q_all.shape[1] // D_HEAD

    for j in range(count):
        page = over_pages[j] if j < over else dec_pages[(j - over) // per, (j - over) % per]
        src = pl.ds(pl.multiple_of(page * PAGE, PAGE), PAGE)
        dst = pl.ds(j * PAGE, PAGE)
        pltpu.make_async_copy(k_hbm.at[src], kbuf.at[dst], sem.at[0]).start()
        pltpu.make_async_copy(v_hbm.at[src], vbuf.at[dst], sem.at[1]).start()

    if batch > over + dec:
        q_all[...] = jnp.zeros_like(q_all)
    q_all[0:over, :] = over_ref[...].astype(jnp.float32)
    q_all[over:over + dec, :] = decq_ref[...].astype(jnp.float32)
    out_ref[...] = jnp.zeros_like(out_ref)
    row = lax.broadcasted_iota(jnp.int32, (batch, PAGE), 0)
    lane = lax.broadcasted_iota(jnp.int32, (batch, PAGE), 1)
    for j in range(count):
        owner, base = (j, 0) if j < over else (over + (j - over) // per, (j - over) % per * PAGE)
        most = over_len[j] if j < over else dec_len[owner - over]
        valid = (row == owner) & (lane + base < most)
        bias[:, j * PAGE:(j + 1) * PAGE] = jnp.where(valid, 0.0, LOW)
    pltpu.make_async_copy(kbuf, kbuf, sem.at[0]).wait()
    pltpu.make_async_copy(vbuf, vbuf, sem.at[1]).wait()

    def head(g, _):
        cols = pl.ds(pl.multiple_of(g * D_HEAD, D_HEAD), D_HEAD)
        q = jnp.concatenate(
            [
                q_all[:, pl.ds(pl.multiple_of((g * GROUP + h) * D_HEAD, D_HEAD), D_HEAD)]
                for h in range(GROUP)
            ],
            axis=0,
        ).astype(jnp.bfloat16)
        s = lax.dot_general(q, kbuf[:, cols], NT, preferred_element_type=jnp.float32)
        s = (s.reshape(GROUP, batch, keys) + bias[...][None]).reshape(GROUP * batch, keys)
        p = jnp.exp2((s - jnp.max(s, axis=1, keepdims=True)) * SCALE)
        w = (p / jnp.sum(p, axis=1, keepdims=True)).astype(jnp.bfloat16)
        o = jnp.dot(w, vbuf[:, cols], preferred_element_type=jnp.float32)
        for h in range(GROUP):
            at = g * GROUP + h
            part = o[h * batch:(h + 1) * batch]
            res[:, pl.ds(pl.multiple_of(at * D_HEAD, D_HEAD), D_HEAD)] = part
            flat[pl.ds(at, batch, stride=heads), :] = part
        return 0

    lax.fori_loop(0, k_hbm.shape[1] // D_HEAD, head, 0)
    dec_ref[...] = res[over:over + dec, :].astype(dec_ref.dtype)
    for m in range(over):
        out_ref[dest_ref[m]] = flat[m * heads:(m + 1) * heads, :].astype(out_ref.dtype)


def small_part(decode_q, overflow_q, keys, values, dec_pages, over_pages, dec_len, over_len, dest, replicas):
    dec, over = decode_q.shape[0], overflow_q.shape[0]
    batch = -(-(dec + over) // 8) * 8
    width = decode_q.shape[1]
    span = (over + dec_pages.size) * PAGE
    work = batch * width * span
    moved = (replicas, width // D_HEAD, D_HEAD)
    return pl.pallas_call(
        small_kernel,
        grid_spec=pltpu.PrefetchScalarGridSpec(
            num_scalar_prefetch=5,
            grid=(1,),
            in_specs=[
                pl.BlockSpec((over, width), lambda i, *_: (0, 0)),
                pl.BlockSpec((dec, width), lambda i, *_: (0, 0)),
                pl.BlockSpec(memory_space=pl.ANY),
                pl.BlockSpec(memory_space=pl.ANY),
            ],
            out_specs=[
                pl.BlockSpec((dec, width), lambda i, *_: (0, 0)),
                pl.BlockSpec(moved, lambda i, *_: (0, 0, 0)),
            ],
            scratch_shapes=[
                pltpu.VMEM((span, keys.shape[1]), jnp.bfloat16),
                pltpu.VMEM((span, keys.shape[1]), jnp.bfloat16),
                pltpu.VMEM((batch, width), jnp.float32),
                pltpu.VMEM((batch, width), jnp.float32),
                pltpu.VMEM((batch, span), jnp.float32),
                pltpu.VMEM((batch * width // D_HEAD, D_HEAD), jnp.float32),
                pltpu.SemaphoreType.DMA((2,)),
            ],
        ),
        out_shape=[
            jax.ShapeDtypeStruct((dec, width), decode_q.dtype),
            jax.ShapeDtypeStruct(moved, decode_q.dtype),
        ],
        compiler_params=pltpu.CompilerParams(vmem_limit_bytes=VMEM_LIMIT),
        cost_estimate=pl.CostEstimate(
            flops=4 * work, bytes_accessed=4 * span * keys.shape[1], transcendentals=work // D_HEAD
        ),
        name="small",
    )(over_pages, dec_pages, over_len, dec_len, dest, overflow_q, decode_q, keys, values)


def finish_kernel(ranks, rank_ref, rows_ref, big_ref, *refs):
    got, (out_ref, mov_ref, flat, sem) = refs[:-4], refs[-4:]
    del big_ref
    cols = got[0].shape[1]
    heads = len(got) // (ranks - 1)
    copies = []
    for i, part in enumerate(got):
        source = lax.rem(rank_ref[0] + ranks - (i // heads + 1), ranks)
        to = pl.ds(pl.multiple_of((source * heads + i % heads) * cols, cols), cols)
        copies.append(pltpu.make_async_copy(part, out_ref.at[:, to], sem.at[i]))
        copies[-1].start()
    replicas, count, _ = rows_ref.shape
    flat[...] = rows_ref[...].astype(jnp.float32).reshape(flat.shape)
    for h in range(count):
        line = flat[pl.ds(h, replicas, stride=count), :]
        mov_ref[:, h * D_HEAD:(h + 1) * D_HEAD] = line.astype(mov_ref.dtype)
    for copy in copies:
        copy.wait()


def finish_part(rank, ranks, rows, big, got):
    replicas, count, _ = rows.shape
    anywhere = pl.BlockSpec(memory_space=pl.ANY)
    return pl.pallas_call(
        functools.partial(finish_kernel, ranks),
        grid_spec=pltpu.PrefetchScalarGridSpec(
            num_scalar_prefetch=1,
            grid=(1,),
            in_specs=[pl.BlockSpec(rows.shape, lambda i, *_: (0, 0, 0)), anywhere]
            + [pl.BlockSpec(memory_space=pltpu.VMEM)] * len(got),
            out_specs=[anywhere, pl.BlockSpec((replicas, count * D_HEAD), lambda i, *_: (0, 0))],
            scratch_shapes=[
                pltpu.VMEM((replicas * count, D_HEAD), jnp.float32),
                pltpu.SemaphoreType.DMA((len(got),)),
            ],
        ),
        out_shape=[
            jax.ShapeDtypeStruct(big.shape, big.dtype),
            jax.ShapeDtypeStruct((replicas, count * D_HEAD), big.dtype),
        ],
        input_output_aliases={2: 0},
        compiler_params=pltpu.CompilerParams(vmem_limit_bytes=16 * 2**20),
        cost_estimate=pl.CostEstimate(
            flops=0, bytes_accessed=2 * big.size + 4 * rows.size, transcendentals=0
        ),
        name="finish",
    )(rank, rows, big, *got)


def per_device(
    prefill_q,
    decode_q,
    overflow_q,
    key_pool,
    value_pool,
    prefill_pages,
    decode_pages,
    decode_len,
    overflow_pages,
    overflow_len,
    overflow_dest,
):
    ranks, replicas = lax.axis_size("tensor"), lax.axis_size("replica")
    rank = lax.axis_index("tensor")
    heads = key_pool.shape[1] // D_HEAD
    pages = prefill_pages[0]

    decode_out, sent = small_part(
        decode_q,
        overflow_q,
        key_pool,
        value_pool,
        decode_pages,
        overflow_pages,
        decode_len,
        overflow_len,
        overflow_dest,
        replicas,
    )
    sent, pages = lax.optimization_barrier((sent, pages))
    rows = lax.all_to_all(sent, "replica", split_axis=0, concat_axis=0, tiled=True)

    got = []
    for shift in range(1, ranks):
        blk = lax.rem(rank + shift, ranks)[None].astype(jnp.int32)
        step = min(heads, 2)
        for g in range(0, heads, step):
            part = prefill_part(
                prefill_q, key_pool, value_pool, pages, blk, ranks, g, step, pack=8
            )
            got.append(lax.ppermute(part, "tensor", [(i, (i + shift) % ranks) for i in range(ranks)]))
    own = rank[None].astype(jnp.int32)
    prefill_out = prefill_part(
        prefill_q, key_pool, value_pool, pages, own, ranks, 0, heads, pack=8, wide=True
    )
    prefill_out, moved_out = finish_part(own, ranks, rows, prefill_out, got)
    return (prefill_out, decode_out, moved_out)


def solution(mesh):
    in_specs = (
        P("replica", "tensor"),
        P("replica", "tensor"),
        P("replica", "tensor"),
        P("replica", "tensor"),
        P("replica", "tensor"),
        P("replica", None),
        P("replica", None),
        P("replica"),
        P("replica"),
        P("replica"),
        P("replica"),
    )
    out_specs = (P(("replica", "tensor"), None), P("replica", "tensor"), P("replica", "tensor"))
    return jax.shard_map(
        per_device, mesh=mesh, in_specs=in_specs, out_specs=out_specs, check_vma=False
    )
```

```python
import functools
import math

import jax
import jax.numpy as jnp
from jax import lax
from jax.experimental import pallas as pl
from jax.experimental.pallas import tpu as pltpu
from jax.sharding import PartitionSpec as P

Q_HEADS = 64
KV_HEADS = 8
D_HEAD = 128
PAGE = 128
GROUP = Q_HEADS // KV_HEADS
SCALE = math.log2(math.e) / math.sqrt(D_HEAD)
LOW = -1e30
CHUNK = 512
VMEM_LIMIT = 60 * 2**20

NT = (((1,), (1,)), ((), ()))


def chunks_of(earlier, tail):
    starts = list(range(0, earlier, CHUNK)) + [earlier]
    return [(a, b - a) for a, b in zip(starts, starts[1:] + [earlier + tail])]


def prefill_kernel(
    tail, blk_ref, pages_ref, q_ref, k_hbm, v_hbm, o_ref,
    kbuf, vbuf, score, top, acc, sem, *, first, pack
):
    heads = kbuf.shape[0]
    count = pages_ref.shape[0]
    span = count * PAGE
    rows = q_ref.shape[0]
    units = GROUP // pack
    pieces = chunks_of(span - tail, tail)

    def fetch(head):
        cols = pl.ds(pl.multiple_of((first + head) * D_HEAD, D_HEAD), D_HEAD)

        for kind, (pool, buf) in enumerate(((k_hbm, kbuf), (v_hbm, vbuf))):
            for i, (start, size) in enumerate(pieces):

                def one(j, _):
                    src = pl.ds(pl.multiple_of(pages_ref[j] * PAGE, PAGE), PAGE)
                    dst = pl.ds(pl.multiple_of(j * PAGE, PAGE), PAGE)
                    pltpu.make_async_copy(
                        pool.at[src, cols], buf.at[head, dst], sem.at[head, kind, i]
                    ).start()
                    return 0

                lax.fori_loop(start // PAGE, (start + size) // PAGE, one, 0)

    def ready(head, kind, i):
        part = (kbuf, vbuf)[kind].at[head, pl.ds(*pieces[i])]
        pltpu.make_async_copy(part, part, sem.at[head, kind, i]).wait()

    def columns(unit, h):
        return pl.ds(pl.multiple_of((unit * pack + h) * D_HEAD, D_HEAD), D_HEAD)

    def across(x, size):
        return jnp.concatenate([x] * (size // D_HEAD), axis=1)

    def fold(op, kept, x):
        for at in range(0, x.shape[1], D_HEAD):
            piece = x[:, at:at + D_HEAD]
            kept = piece if kept is None else op(kept, piece)
        return kept

    def tops(u):
        return pl.when(u >= 0)

    def unit(u, _):
        head = u // units

        @pl.when((u % units == 0) & (head + 1 < heads))
        def _():
            fetch(head + 1)

        for i, (start, size) in enumerate(pieces):

            @pl.when(u % units == 0)
            def _(i=i):
                ready(head, 0, i)

            @tops(u)
            def _(i=i, start=start, size=size):
                q = jnp.concatenate([q_ref[:, columns(u, h)] for h in range(pack)], axis=0)
                keys = kbuf[head, start:start + size, :]
                s = lax.dot_general(q, keys, NT, preferred_element_type=jnp.float32)
                if start >= span - tail:
                    usable = lax.broadcasted_iota(jnp.int32, (rows, size), 1) <= (
                        lax.broadcasted_iota(jnp.int32, (rows, size), 0)
                        + (blk_ref[0] * rows + span - tail - start)
                    )
                    s = jnp.where(usable[None], s.reshape(pack, rows, size), LOW).reshape(s.shape)
                score[:, start:start + size] = s
                peak = fold(jnp.maximum, None, s)
                if i > 0:
                    peak = jnp.maximum(peak, top[...])
                if start + size == span:
                    peak = jnp.max(peak, axis=1, keepdims=True) * SCALE
                    peak = jnp.broadcast_to(peak, top.shape)
                top[...] = peak

        for i, (start, size) in enumerate(pieces):

            @pl.when(u % units == 0)
            def _(i=i):
                ready(head, 1, i)

            @tops(u)
            def _(i=i, start=start, size=size):
                x = score[:, start:start + size]
                p = jnp.exp2(x * SCALE - across(top[...], size))
                values = vbuf[head, start:start + size, :]
                values = jnp.concatenate([values, jnp.ones_like(values)], axis=1)
                o = jnp.dot(p.astype(jnp.bfloat16), values, preferred_element_type=jnp.float32)
                if i > 0:
                    o = o + acc[...]
                if start + size < span:
                    acc[...] = o
                else:
                    o = (o[:, :D_HEAD] / o[:, D_HEAD:]).astype(o_ref.dtype)
                    for h in range(pack):
                        o_ref[:, columns(u, h)] = o[h * rows:(h + 1) * rows]

        return 0

    fetch(0)
    lax.fori_loop(0, heads * units, unit, 0)


def prefill_part(q, keys, values, pages, blk, ranks, first, heads, pack, wide=False):
    tokens = q.shape[0]
    rows = tokens // ranks
    span = pages.shape[0] * PAGE
    width = heads * GROUP * D_HEAD
    total = ranks * keys.shape[1] // D_HEAD // heads if wide else 1
    work = heads * GROUP * rows * span

    return pl.pallas_call(
        functools.partial(prefill_kernel, tokens, first=first, pack=pack),
        grid_spec=pltpu.PrefetchScalarGridSpec(
            num_scalar_prefetch=2,
            grid=(1,),
            in_specs=[
                pl.BlockSpec((rows, width), lambda i, blk, pages: (blk[0], first // heads)),
                pl.BlockSpec(memory_space=pl.ANY),
                pl.BlockSpec(memory_space=pl.ANY),
            ],
            out_specs=pl.BlockSpec((rows, width), lambda i, blk, pages: (0, blk[0] if wide else 0)),
            scratch_shapes=[
                pltpu.VMEM((heads, span, D_HEAD), jnp.bfloat16),
                pltpu.VMEM((heads, span, D_HEAD), jnp.bfloat16),
                pltpu.VMEM((pack * rows, span), jnp.float32),
                pltpu.VMEM((pack * rows, D_HEAD), jnp.float32),
                pltpu.VMEM((pack * rows, 2 * D_HEAD), jnp.float32),
                pltpu.SemaphoreType.DMA((heads, 2, len(chunks_of(span - tokens, tokens)))),
            ],
        ),
        out_shape=jax.ShapeDtypeStruct((rows, total * width), q.dtype),
        compiler_params=pltpu.CompilerParams(vmem_limit_bytes=VMEM_LIMIT),
        cost_estimate=pl.CostEstimate(
            flops=4 * work * D_HEAD,
            bytes_accessed=4 * (heads * span * D_HEAD + rows * width),
            transcendentals=work,
        ),
        name="prefill",
    )(blk, pages, q, keys, values)


def small_kernel(
    over_pages, dec_pages, over_len, dec_len, dest_ref, over_ref, decq_ref, k_hbm, v_hbm,
    dec_ref, out_ref, kbuf, vbuf, q_all, res, flat, sem
):
    over, (dec, per) = over_pages.shape[0], dec_pages.shape
    count = over + dec * per
    batch = q_all.shape[0]
    keys = count * PAGE
    heads = q_all.shape[1] // D_HEAD

    for kind, (pool, buf) in enumerate(((k_hbm, kbuf), (v_hbm, vbuf))):
        for j in range(count):
            page = over_pages[j] if j < over else dec_pages[(j - over) // per, (j - over) % per]
            src = pl.ds(pl.multiple_of(page * PAGE, PAGE), PAGE)
            pltpu.make_async_copy(
                pool.at[src], buf.at[pl.ds(j * PAGE, PAGE)], sem.at[kind]
            ).start()

    if batch > over + dec:
        q_all[...] = jnp.zeros_like(q_all)
    q_all[0:over, :] = over_ref[...].astype(jnp.float32)
    q_all[over:over + dec, :] = decq_ref[...].astype(jnp.float32)
    out_ref[...] = jnp.zeros_like(out_ref)
    row = lax.broadcasted_iota(jnp.int32, (batch, PAGE), 0)
    lane = lax.broadcasted_iota(jnp.int32, (batch, PAGE), 1)
    masks = []
    for j in range(count):
        owner, base = (j, 0) if j < over else (over + (j - over) // per, (j - over) % per * PAGE)
        most = over_len[j] if j < over else dec_len[owner - over]
        masks.append((row == owner) & (lane + base < most))
    pltpu.make_async_copy(kbuf, kbuf, sem.at[0]).wait()
    for g in range(k_hbm.shape[1] // D_HEAD):
        cols = slice(g * D_HEAD, (g + 1) * D_HEAD)
        q = jnp.concatenate(
            [q_all[:, (g * GROUP + h) * D_HEAD:(g * GROUP + h + 1) * D_HEAD] for h in range(GROUP)],
            axis=0,
        ).astype(jnp.bfloat16)
        s = lax.dot_general(q, kbuf[:, cols], NT, preferred_element_type=jnp.float32)
        s = s.reshape(GROUP, batch, keys)
        s = jnp.concatenate(
            [
                jnp.where(masks[j][None], s[:, :, j * PAGE:(j + 1) * PAGE], LOW)
                for j in range(count)
            ],
            axis=2,
        ).reshape(GROUP * batch, keys)
        p = jnp.exp2((s - jnp.max(s, axis=1, keepdims=True)) * SCALE)
        total = jnp.sum(p, axis=1, keepdims=True)
        w = (p / total).astype(jnp.bfloat16)
        if g == 0:
            pltpu.make_async_copy(vbuf, vbuf, sem.at[1]).wait()
        o = jnp.dot(w, vbuf[:, cols], preferred_element_type=jnp.float32)
        for h in range(GROUP):
            at = g * GROUP + h
            res[:, at * D_HEAD:(at + 1) * D_HEAD] = o[h * batch:(h + 1) * batch]
            flat[pl.ds(at, batch, stride=heads), :] = o[h * batch:(h + 1) * batch]
    dec_ref[...] = res[over:over + dec, :].astype(dec_ref.dtype)
    for m in range(over):
        out_ref[dest_ref[m]] = flat[m * heads:(m + 1) * heads, :].astype(out_ref.dtype)


def small_part(decode_q, overflow_q, keys, values, dec_pages, over_pages, dec_len, over_len, dest, replicas):
    dec, over = decode_q.shape[0], overflow_q.shape[0]
    batch = -(-(dec + over) // 8) * 8
    width = decode_q.shape[1]
    span = (over + dec_pages.size) * PAGE
    work = batch * width * span
    moved = (replicas, width // D_HEAD, D_HEAD)
    return pl.pallas_call(
        small_kernel,
        grid_spec=pltpu.PrefetchScalarGridSpec(
            num_scalar_prefetch=5,
            grid=(1,),
            in_specs=[
                pl.BlockSpec((over, width), lambda i, *_: (0, 0)),
                pl.BlockSpec((dec, width), lambda i, *_: (0, 0)),
                pl.BlockSpec(memory_space=pl.ANY),
                pl.BlockSpec(memory_space=pl.ANY),
            ],
            out_specs=[
                pl.BlockSpec((dec, width), lambda i, *_: (0, 0)),
                pl.BlockSpec(moved, lambda i, *_: (0, 0, 0)),
            ],
            scratch_shapes=[
                pltpu.VMEM((span, keys.shape[1]), jnp.bfloat16),
                pltpu.VMEM((span, keys.shape[1]), jnp.bfloat16),
                pltpu.VMEM((batch, width), jnp.float32),
                pltpu.VMEM((batch, width), jnp.float32),
                pltpu.VMEM((batch * width // D_HEAD, D_HEAD), jnp.float32),
                pltpu.SemaphoreType.DMA((2,)),
            ],
        ),
        out_shape=[
            jax.ShapeDtypeStruct((dec, width), decode_q.dtype),
            jax.ShapeDtypeStruct(moved, decode_q.dtype),
        ],
        compiler_params=pltpu.CompilerParams(vmem_limit_bytes=VMEM_LIMIT),
        cost_estimate=pl.CostEstimate(
            flops=4 * work, bytes_accessed=4 * span * keys.shape[1], transcendentals=work // D_HEAD
        ),
        name="small",
    )(over_pages, dec_pages, over_len, dec_len, dest, overflow_q, decode_q, keys, values)


def finish_kernel(ranks, rank_ref, rows_ref, big_ref, *refs):
    got, (out_ref, mov_ref, flat, sem) = refs[:-4], refs[-4:]
    del big_ref
    cols = got[0].shape[1]
    heads = len(got) // (ranks - 1)
    copies = []
    for i, part in enumerate(got):
        source = lax.rem(rank_ref[0] + ranks - (i // heads + 1), ranks)
        to = pl.ds(pl.multiple_of((source * heads + i % heads) * cols, cols), cols)
        copies.append(pltpu.make_async_copy(part, out_ref.at[:, to], sem.at[i]))
        copies[-1].start()
    replicas, count, _ = rows_ref.shape
    flat[...] = rows_ref[...].astype(jnp.float32).reshape(flat.shape)
    for h in range(count):
        line = flat[pl.ds(h, replicas, stride=count), :]
        mov_ref[:, h * D_HEAD:(h + 1) * D_HEAD] = line.astype(mov_ref.dtype)
    for copy in copies:
        copy.wait()


def finish_part(rank, ranks, rows, big, got):
    replicas, count, _ = rows.shape
    anywhere = pl.BlockSpec(memory_space=pl.ANY)
    return pl.pallas_call(
        functools.partial(finish_kernel, ranks),
        grid_spec=pltpu.PrefetchScalarGridSpec(
            num_scalar_prefetch=1,
            grid=(1,),
            in_specs=[pl.BlockSpec(rows.shape, lambda i, *_: (0, 0, 0)), anywhere]
            + [pl.BlockSpec(memory_space=pltpu.VMEM)] * len(got),
            out_specs=[anywhere, pl.BlockSpec((replicas, count * D_HEAD), lambda i, *_: (0, 0))],
            scratch_shapes=[
                pltpu.VMEM((replicas * count, D_HEAD), jnp.float32),
                pltpu.SemaphoreType.DMA((len(got),)),
            ],
        ),
        out_shape=[
            jax.ShapeDtypeStruct(big.shape, big.dtype),
            jax.ShapeDtypeStruct((replicas, count * D_HEAD), big.dtype),
        ],
        input_output_aliases={2: 0},
        compiler_params=pltpu.CompilerParams(vmem_limit_bytes=16 * 2**20),
        cost_estimate=pl.CostEstimate(
            flops=0, bytes_accessed=2 * big.size + 4 * rows.size, transcendentals=0
        ),
        name="finish",
    )(rank, rows, big, *got)


def per_device(
    prefill_q,
    decode_q,
    overflow_q,
    key_pool,
    value_pool,
    prefill_pages,
    decode_pages,
    decode_len,
    overflow_pages,
    overflow_len,
    overflow_dest,
):
    ranks, replicas = lax.axis_size("tensor"), lax.axis_size("replica")
    rank = lax.axis_index("tensor")
    heads = key_pool.shape[1] // D_HEAD
    pages = prefill_pages[0]

    decode_out, sent = small_part(
        decode_q,
        overflow_q,
        key_pool,
        value_pool,
        decode_pages,
        overflow_pages,
        decode_len,
        overflow_len,
        overflow_dest,
        replicas,
    )
    sent, pages = lax.optimization_barrier((sent, pages))
    rows = lax.all_to_all(sent, "replica", split_axis=0, concat_axis=0, tiled=True)

    got = []
    for shift in range(1, ranks):
        blk = lax.rem(rank + shift, ranks)[None].astype(jnp.int32)
        step = min(heads, 2)
        for g in range(0, heads, step):
            part = prefill_part(
                prefill_q, key_pool, value_pool, pages, blk, ranks, g, step, pack=8
            )
            got.append(lax.ppermute(part, "tensor", [(i, (i + shift) % ranks) for i in range(ranks)]))
    own = rank[None].astype(jnp.int32)
    prefill_out = prefill_part(
        prefill_q, key_pool, value_pool, pages, own, ranks, 0, heads, pack=8, wide=True
    )
    prefill_out, moved_out = finish_part(own, ranks, rows, prefill_out, got)
    return (prefill_out, decode_out, moved_out)


def solution(mesh):
    in_specs = (
        P("replica", "tensor"),
        P("replica", "tensor"),
        P("replica", "tensor"),
        P("replica", "tensor"),
        P("replica", "tensor"),
        P("replica", None),
        P("replica", None),
        P("replica"),
        P("replica"),
        P("replica"),
        P("replica"),
    )
    out_specs = (P(("replica", "tensor"), None), P("replica", "tensor"), P("replica", "tensor"))
    return jax.shard_map(
        per_device, mesh=mesh, in_specs=in_specs, out_specs=out_specs, check_vma=False
    )
```

```python
import functools
import math

import jax
import jax.numpy as jnp
from jax import lax
from jax.experimental import pallas as pl
from jax.experimental.pallas import tpu as pltpu
from jax.sharding import PartitionSpec as P

Q_HEADS = 64
KV_HEADS = 8
D_HEAD = 128
PAGE = 128
GROUP = Q_HEADS // KV_HEADS
SCALE = math.log2(math.e) / math.sqrt(D_HEAD)
LOW = -1e30
CHUNK = 512
VMEM_LIMIT = 60 * 2**20

NT = (((1,), (1,)), ((), ()))


def chunks_of(earlier, tail):
    starts = list(range(0, earlier, CHUNK)) + [earlier]
    return [(a, b - a) for a, b in zip(starts, starts[1:] + [earlier + tail])]


def prefill_kernel(
    tail, blk_ref, pages_ref, q_ref, k_hbm, v_hbm, o_ref,
    kbuf, vbuf, score, top, acc, sem, *, first, pack
):
    heads = kbuf.shape[0]
    count = pages_ref.shape[0]
    span = count * PAGE
    rows = q_ref.shape[0]
    units = GROUP // pack
    pieces = chunks_of(span - tail, tail)

    def fetch(head):
        cols = pl.ds(pl.multiple_of((first + head) * D_HEAD, D_HEAD), D_HEAD)

        for kind, (pool, buf) in enumerate(((k_hbm, kbuf), (v_hbm, vbuf))):

            def one(j, _):
                src = pl.ds(pl.multiple_of(pages_ref[j] * PAGE, PAGE), PAGE)
                dst = pl.ds(pl.multiple_of(j * PAGE, PAGE), PAGE)
                pltpu.make_async_copy(
                    pool.at[src, cols], buf.at[head, dst], sem.at[head, kind]
                ).start()
                return 0

            lax.fori_loop(0, count, one, 0)

    def keys_ready(head):
        pltpu.make_async_copy(kbuf.at[head], kbuf.at[head], sem.at[head, 0]).wait()

    def values_ready(head):
        pltpu.make_async_copy(vbuf.at[head], vbuf.at[head], sem.at[head, 1]).wait()

    def columns(unit, h):
        return pl.ds(pl.multiple_of((unit * pack + h) * D_HEAD, D_HEAD), D_HEAD)

    def across(x, size):
        return jnp.concatenate([x] * (size // D_HEAD), axis=1)

    def fold(op, kept, x):
        for at in range(0, x.shape[1], D_HEAD):
            piece = x[:, at:at + D_HEAD]
            kept = piece if kept is None else op(kept, piece)
        return kept

    def tops(u):
        return pl.when(u >= 0)

    def unit(u, _):
        head = u // units

        @pl.when((u % units == 0) & (head + 1 < heads))
        def _():
            fetch(head + 1)

        @pl.when(u % units == 0)
        def _():
            keys_ready(head)

        for i, (start, size) in enumerate(pieces):

            @tops(u)
            def _(i=i, start=start, size=size):
                q = jnp.concatenate([q_ref[:, columns(u, h)] for h in range(pack)], axis=0)
                keys = kbuf[head, start:start + size, :]
                s = lax.dot_general(q, keys, NT, preferred_element_type=jnp.float32)
                if start >= span - tail:
                    usable = lax.broadcasted_iota(jnp.int32, (rows, size), 1) <= (
                        lax.broadcasted_iota(jnp.int32, (rows, size), 0)
                        + (blk_ref[0] * rows + span - tail - start)
                    )
                    s = jnp.where(usable[None], s.reshape(pack, rows, size), LOW).reshape(s.shape)
                score[:, start:start + size] = s
                peak = fold(jnp.maximum, None, s)
                if i > 0:
                    peak = jnp.maximum(peak, top[...])
                if start + size == span:
                    peak = jnp.max(peak, axis=1, keepdims=True) * SCALE
                    peak = jnp.broadcast_to(peak, top.shape)
                top[...] = peak

        @pl.when(u % units == 0)
        def _():
            values_ready(head)

        for i, (start, size) in enumerate(pieces):

            @tops(u)
            def _(i=i, start=start, size=size):
                x = score[:, start:start + size]
                p = jnp.exp2(x * SCALE - across(top[...], size))
                values = vbuf[head, start:start + size, :]
                values = jnp.concatenate([values, jnp.ones_like(values)], axis=1)
                o = jnp.dot(p.astype(jnp.bfloat16), values, preferred_element_type=jnp.float32)
                if i > 0:
                    o = o + acc[...]
                if start + size < span:
                    acc[...] = o
                else:
                    o = (o[:, :D_HEAD] / o[:, D_HEAD:]).astype(o_ref.dtype)
                    for h in range(pack):
                        o_ref[:, columns(u, h)] = o[h * rows:(h + 1) * rows]

        return 0

    fetch(0)
    lax.fori_loop(0, heads * units, unit, 0)


def prefill_part(q, keys, values, pages, blk, ranks, first, heads, pack, wide=False):
    tokens = q.shape[0]
    rows = tokens // ranks
    span = pages.shape[0] * PAGE
    width = heads * GROUP * D_HEAD
    total = ranks * keys.shape[1] // D_HEAD // heads if wide else 1
    work = heads * GROUP * rows * span

    return pl.pallas_call(
        functools.partial(prefill_kernel, tokens, first=first, pack=pack),
        grid_spec=pltpu.PrefetchScalarGridSpec(
            num_scalar_prefetch=2,
            grid=(1,),
            in_specs=[
                pl.BlockSpec((rows, width), lambda i, blk, pages: (blk[0], first // heads)),
                pl.BlockSpec(memory_space=pl.ANY),
                pl.BlockSpec(memory_space=pl.ANY),
            ],
            out_specs=pl.BlockSpec((rows, width), lambda i, blk, pages: (0, blk[0] if wide else 0)),
            scratch_shapes=[
                pltpu.VMEM((heads, span, D_HEAD), jnp.bfloat16),
                pltpu.VMEM((heads, span, D_HEAD), jnp.bfloat16),
                pltpu.VMEM((pack * rows, span), jnp.float32),
                pltpu.VMEM((pack * rows, D_HEAD), jnp.float32),
                pltpu.VMEM((pack * rows, 2 * D_HEAD), jnp.float32),
                pltpu.SemaphoreType.DMA((heads, 2)),
            ],
        ),
        out_shape=jax.ShapeDtypeStruct((rows, total * width), q.dtype),
        compiler_params=pltpu.CompilerParams(vmem_limit_bytes=VMEM_LIMIT),
        cost_estimate=pl.CostEstimate(
            flops=4 * work * D_HEAD,
            bytes_accessed=4 * (heads * span * D_HEAD + rows * width),
            transcendentals=work,
        ),
        name="prefill",
    )(blk, pages, q, keys, values)


def small_kernel(
    over_pages, dec_pages, over_len, dec_len, dest_ref, over_ref, decq_ref, k_hbm, v_hbm,
    dec_ref, out_ref, kbuf, vbuf, q_all, res, flat, sem
):
    over, (dec, per) = over_pages.shape[0], dec_pages.shape
    count = over + dec * per
    batch = q_all.shape[0]
    keys = count * PAGE
    heads = q_all.shape[1] // D_HEAD

    for kind, (pool, buf) in enumerate(((k_hbm, kbuf), (v_hbm, vbuf))):
        for j in range(count):
            page = over_pages[j] if j < over else dec_pages[(j - over) // per, (j - over) % per]
            src = pl.ds(pl.multiple_of(page * PAGE, PAGE), PAGE)
            pltpu.make_async_copy(
                pool.at[src], buf.at[pl.ds(j * PAGE, PAGE)], sem.at[kind]
            ).start()

    if batch > over + dec:
        q_all[...] = jnp.zeros_like(q_all)
    q_all[0:over, :] = over_ref[...].astype(jnp.float32)
    q_all[over:over + dec, :] = decq_ref[...].astype(jnp.float32)
    out_ref[...] = jnp.zeros_like(out_ref)
    row = lax.broadcasted_iota(jnp.int32, (batch, PAGE), 0)
    lane = lax.broadcasted_iota(jnp.int32, (batch, PAGE), 1)
    masks = []
    for j in range(count):
        owner, base = (j, 0) if j < over else (over + (j - over) // per, (j - over) % per * PAGE)
        most = over_len[j] if j < over else dec_len[owner - over]
        masks.append((row == owner) & (lane + base < most))
    pltpu.make_async_copy(kbuf, kbuf, sem.at[0]).wait()
    for g in range(k_hbm.shape[1] // D_HEAD):
        cols = slice(g * D_HEAD, (g + 1) * D_HEAD)
        q = jnp.concatenate(
            [q_all[:, (g * GROUP + h) * D_HEAD:(g * GROUP + h + 1) * D_HEAD] for h in range(GROUP)],
            axis=0,
        ).astype(jnp.bfloat16)
        s = lax.dot_general(q, kbuf[:, cols], NT, preferred_element_type=jnp.float32)
        s = s.reshape(GROUP, batch, keys)
        s = jnp.concatenate(
            [
                jnp.where(masks[j][None], s[:, :, j * PAGE:(j + 1) * PAGE], LOW)
                for j in range(count)
            ],
            axis=2,
        ).reshape(GROUP * batch, keys)
        p = jnp.exp2((s - jnp.max(s, axis=1, keepdims=True)) * SCALE)
        total = jnp.sum(p, axis=1, keepdims=True)
        w = (p / total).astype(jnp.bfloat16)
        if g == 0:
            pltpu.make_async_copy(vbuf, vbuf, sem.at[1]).wait()
        o = jnp.dot(w, vbuf[:, cols], preferred_element_type=jnp.float32)
        for h in range(GROUP):
            at = g * GROUP + h
            res[:, at * D_HEAD:(at + 1) * D_HEAD] = o[h * batch:(h + 1) * batch]
            flat[pl.ds(at, batch, stride=heads), :] = o[h * batch:(h + 1) * batch]
    dec_ref[...] = res[over:over + dec, :].astype(dec_ref.dtype)
    for m in range(over):
        out_ref[dest_ref[m]] = flat[m * heads:(m + 1) * heads, :].astype(out_ref.dtype)


def small_part(decode_q, overflow_q, keys, values, dec_pages, over_pages, dec_len, over_len, dest, replicas):
    dec, over = decode_q.shape[0], overflow_q.shape[0]
    batch = -(-(dec + over) // 8) * 8
    width = decode_q.shape[1]
    span = (over + dec_pages.size) * PAGE
    work = batch * width * span
    moved = (replicas, width // D_HEAD, D_HEAD)
    return pl.pallas_call(
        small_kernel,
        grid_spec=pltpu.PrefetchScalarGridSpec(
            num_scalar_prefetch=5,
            grid=(1,),
            in_specs=[
                pl.BlockSpec((over, width), lambda i, *_: (0, 0)),
                pl.BlockSpec((dec, width), lambda i, *_: (0, 0)),
                pl.BlockSpec(memory_space=pl.ANY),
                pl.BlockSpec(memory_space=pl.ANY),
            ],
            out_specs=[
                pl.BlockSpec((dec, width), lambda i, *_: (0, 0)),
                pl.BlockSpec(moved, lambda i, *_: (0, 0, 0)),
            ],
            scratch_shapes=[
                pltpu.VMEM((span, keys.shape[1]), jnp.bfloat16),
                pltpu.VMEM((span, keys.shape[1]), jnp.bfloat16),
                pltpu.VMEM((batch, width), jnp.float32),
                pltpu.VMEM((batch, width), jnp.float32),
                pltpu.VMEM((batch * width // D_HEAD, D_HEAD), jnp.float32),
                pltpu.SemaphoreType.DMA((2,)),
            ],
        ),
        out_shape=[
            jax.ShapeDtypeStruct((dec, width), decode_q.dtype),
            jax.ShapeDtypeStruct(moved, decode_q.dtype),
        ],
        compiler_params=pltpu.CompilerParams(vmem_limit_bytes=VMEM_LIMIT),
        cost_estimate=pl.CostEstimate(
            flops=4 * work, bytes_accessed=4 * span * keys.shape[1], transcendentals=work // D_HEAD
        ),
        name="small",
    )(over_pages, dec_pages, over_len, dec_len, dest, overflow_q, decode_q, keys, values)


def finish_kernel(ranks, rank_ref, rows_ref, big_ref, *refs):
    got, (out_ref, mov_ref, flat, sem) = refs[:-4], refs[-4:]
    del big_ref
    cols = got[0].shape[1]
    heads = len(got) // (ranks - 1)
    copies = []
    for i, part in enumerate(got):
        source = lax.rem(rank_ref[0] + ranks - (i // heads + 1), ranks)
        to = pl.ds(pl.multiple_of((source * heads + i % heads) * cols, cols), cols)
        copies.append(pltpu.make_async_copy(part, out_ref.at[:, to], sem.at[i]))
        copies[-1].start()
    replicas, count, _ = rows_ref.shape
    flat[...] = rows_ref[...].astype(jnp.float32).reshape(flat.shape)
    for h in range(count):
        line = flat[pl.ds(h, replicas, stride=count), :]
        mov_ref[:, h * D_HEAD:(h + 1) * D_HEAD] = line.astype(mov_ref.dtype)
    for copy in copies:
        copy.wait()


def finish_part(rank, ranks, rows, big, got):
    replicas, count, _ = rows.shape
    anywhere = pl.BlockSpec(memory_space=pl.ANY)
    return pl.pallas_call(
        functools.partial(finish_kernel, ranks),
        grid_spec=pltpu.PrefetchScalarGridSpec(
            num_scalar_prefetch=1,
            grid=(1,),
            in_specs=[pl.BlockSpec(rows.shape, lambda i, *_: (0, 0, 0)), anywhere]
            + [pl.BlockSpec(memory_space=pltpu.VMEM)] * len(got),
            out_specs=[anywhere, pl.BlockSpec((replicas, count * D_HEAD), lambda i, *_: (0, 0))],
            scratch_shapes=[
                pltpu.VMEM((replicas * count, D_HEAD), jnp.float32),
                pltpu.SemaphoreType.DMA((len(got),)),
            ],
        ),
        out_shape=[
            jax.ShapeDtypeStruct(big.shape, big.dtype),
            jax.ShapeDtypeStruct((replicas, count * D_HEAD), big.dtype),
        ],
        input_output_aliases={2: 0},
        compiler_params=pltpu.CompilerParams(vmem_limit_bytes=16 * 2**20),
        cost_estimate=pl.CostEstimate(
            flops=0, bytes_accessed=2 * big.size + 4 * rows.size, transcendentals=0
        ),
        name="finish",
    )(rank, rows, big, *got)


def per_device(
    prefill_q,
    decode_q,
    overflow_q,
    key_pool,
    value_pool,
    prefill_pages,
    decode_pages,
    decode_len,
    overflow_pages,
    overflow_len,
    overflow_dest,
):
    ranks, replicas = lax.axis_size("tensor"), lax.axis_size("replica")
    rank = lax.axis_index("tensor")
    heads = key_pool.shape[1] // D_HEAD
    pages = prefill_pages[0]

    decode_out, sent = small_part(
        decode_q,
        overflow_q,
        key_pool,
        value_pool,
        decode_pages,
        overflow_pages,
        decode_len,
        overflow_len,
        overflow_dest,
        replicas,
    )
    sent, pages = lax.optimization_barrier((sent, pages))
    rows = lax.all_to_all(sent, "replica", split_axis=0, concat_axis=0, tiled=True)

    got = []
    for shift in range(1, ranks):
        blk = lax.rem(rank + shift, ranks)[None].astype(jnp.int32)
        step = min(heads, 2)
        for g in range(0, heads, step):
            part = prefill_part(
                prefill_q, key_pool, value_pool, pages, blk, ranks, g, step, pack=8
            )
            got.append(lax.ppermute(part, "tensor", [(i, (i + shift) % ranks) for i in range(ranks)]))
    own = rank[None].astype(jnp.int32)
    prefill_out = prefill_part(
        prefill_q, key_pool, value_pool, pages, own, ranks, 0, heads, pack=8, wide=True
    )
    prefill_out, moved_out = finish_part(own, ranks, rows, prefill_out, got)
    return (prefill_out, decode_out, moved_out)


def solution(mesh):
    in_specs = (
        P("replica", "tensor"),
        P("replica", "tensor"),
        P("replica", "tensor"),
        P("replica", "tensor"),
        P("replica", "tensor"),
        P("replica", None),
        P("replica", None),
        P("replica"),
        P("replica"),
        P("replica"),
        P("replica"),
    )
    out_specs = (P(("replica", "tensor"), None), P("replica", "tensor"), P("replica", "tensor"))
    return jax.shard_map(
        per_device, mesh=mesh, in_specs=in_specs, out_specs=out_specs, check_vma=False
    )
```
